32 devices in a mesh: lat: 4 (over y, x), lon: 4 (over z), lev: 2 (over core).
Axes of the slice: x: 2, y: 2, z: 4, core: 2. Of those that a mesh axis runs over, the one named last changes fastest.
Arguments:
- ensemble: float32 [80, 6, 2, 32, 512], P(None, None, 'lev', 'lat', 'lon'), may hold values from -6 to 6
- obs_values: float32 [2, 2048], replicated, may hold values from -6 to 6
- obs_error_var: float32 [2, 2048], replicated, may hold values from 0.25 to 2
- obs_lat: int32 [2, 2048], replicated, may hold values from 0 to 30
- obs_lon: int32 [2, 2048], replicated, may hold values from 0 to 511
- obs_level: int32 [2, 2048], replicated, may hold values from 0 to 11
- obs_frac: float32 [2, 2, 2048], replicated, may hold values from 0 to 1
- loc_mask: int32 [2, 16, 6, 2, 32, 4], P(None, None, None, 'lev', 'lat', 'lon'), may hold values 0 or 1
Outputs:
- analysis: float32 [80, 6, 2, 32, 512], P(None, None, 'lev', 'lat', 'lon')
- prior_stats: float32 [2, 2, 2048], replicated
- posterior_stats: float32 [2, 2, 2048], replicated
The draws below stay inside these ranges and needn't reach their ends.
Inputs may be any that keep to these rules, and one draw needn't show every extreme that they name: `obs_lat`: every stencil lies inside the grid's rows.
All inputs are finite; a program needn't handle non-finite values. No bound on the sum of `loc_mask` on one device may be relied on, other than what follows from the above.
Results may differ from the reference program's by a relative error of at most 0.0003.
Values sent between devices are 32-bit elements; how exact they have to be, the bound alone decides.
No kernel may reach another device: no remote copies, remote signals or barrier semaphores. Data moves between devices by JAX's collectives and lax.ppermute only.
A program may use at most 64 MiB of HBM per device.

```python
import math
import jax
import jax.numpy as jnp
from jax import lax

M = 80
VARS = 6
CLAT = 8
CLON = 128
OBLK = 128
BLOCKS = 16
BATCHES = 2
LEVELS = 2
NLAT = 32
NLON = 512
NOBS = 2048
N_LON = 4


def touch_ends(values, key, low, top_value):
    shape = values.shape
    index_at = [jax.random.randint(jax.random.fold_in(key, axis), (), 0, shape[axis]) for axis in range(len(shape))]
    values = values.at[tuple(index_at)].set(low)
    longest = shape.index(max(shape))
    index_at[longest] = (index_at[longest] + 1) % shape[longest]
    return values.at[tuple(index_at)].set(top_value)


def block_scale(stream_key, dims, cuts, smallest, largest):
    loudness, own = 1.0, jax.random.fold_in(stream_key, 6)
    for dim, shards_of in cuts:
        draws = jnp.exp(jax.random.uniform(jax.random.fold_in(own, dim), (shards_of,), jnp.float32, smallest / len(cuts), largest / len(cuts)))
        loudness = loudness * jnp.repeat(draws, dims[dim] // shards_of).reshape([-1 if axis == dim else 1 for axis in range(len(dims))])
    return loudness


def noise(key, extent, spread, bound, shards=(), kind=jnp.bfloat16):
    entries = spread * jax.random.normal(key, extent, jnp.float32)
    if shards:
        entries = entries * block_scale(key, extent, shards, -0.22, 0.18)
    return jnp.clip(entries, -bound, bound).astype(kind)


def setup_inputs(seed: int = 0) -> dict:
    seeds = jax.random.split(jax.random.key(seed), 9)
    ensemble = noise(seeds[0], (M, VARS, LEVELS, NLAT, NLON), 1.0, 6.0, ((2, 2), (3, 4), (4, 4)), jnp.float32)
    obs_values = noise(seeds[1], (BATCHES, NOBS), 1.0, 6.0, (), jnp.float32)
    obs_error_var = jnp.clip(jnp.exp(jax.random.uniform(seeds[2], (BATCHES, NOBS), jnp.float32, math.log(0.25), math.log(2.0))), 0.25, 2.0)
    obs_lat = touch_ends(jax.random.randint(seeds[3], (BATCHES, NOBS), 0, NLAT - 1), jax.random.fold_in(seeds[3], 1), 0, (NLAT - 1) - 1).astype(jnp.int32)
    obs_lon = touch_ends(jax.random.randint(seeds[4], (BATCHES, NOBS), 0, NLON), jax.random.fold_in(seeds[4], 1), 0, NLON - 1).astype(jnp.int32)
    obs_level = touch_ends(jax.random.randint(seeds[5], (BATCHES, NOBS), 0, VARS * LEVELS), jax.random.fold_in(seeds[5], 1), 0, (VARS * LEVELS) - 1).astype(jnp.int32)
    obs_frac = jnp.clip(jax.random.uniform(seeds[6], (BATCHES, 2, NOBS), jnp.float32, 0.0, 1.0), 0.0, 1.0)
    loc_mask = touch_ends((jax.random.randint(seeds[7], (BATCHES, BLOCKS, VARS, LEVELS, NLAT, N_LON), 0, 4) < 3).astype(jnp.int32), jax.random.fold_in(seeds[7], 1), 0, 1)
    return dict(ensemble=ensemble, obs_values=obs_values, obs_error_var=obs_error_var, obs_lat=obs_lat, obs_lon=obs_lon, obs_level=obs_level, obs_frac=obs_frac, loc_mask=loc_mask)


epsilon = 1e-06

def forward(state_rows, lat_rows, lon_cols, level_ids, fraction):
    lat_fraction = fraction[0]
    lon_fraction = fraction[1]
    first_row = (level_ids * NLAT + lat_rows) * NLON
    second_row = first_row + NLON
    second_col = (lon_cols + 1) % NLON
    result = (1.0 - lat_fraction) * (1.0 - lon_fraction) * state_rows[:, first_row + lon_cols]
    result = result + lat_fraction * (1.0 - lon_fraction) * state_rows[:, second_row + lon_cols]
    result = result + (1.0 - lat_fraction) * lon_fraction * state_rows[:, first_row + second_col]
    result = result + lat_fraction * lon_fraction * state_rows[:, second_row + second_col]
    return result

def spread_stats(ensemble_obs):
    center = lax.optimization_barrier(jnp.mean(ensemble_obs, axis=0))
    anomaly = ensemble_obs - center
    variance = lax.optimization_barrier(jnp.sum(anomaly * anomaly, axis=0)) / (ensemble_obs.shape[0] - 1) + epsilon
    return jnp.stack([center, jnp.sqrt(variance)])

def adjust(prior_obs, obs_value, error_var):
    center = lax.optimization_barrier(jnp.mean(prior_obs, axis=0))
    anomaly = prior_obs - center
    variance = lax.optimization_barrier(jnp.sum(anomaly * anomaly, axis=0)) / (prior_obs.shape[0] - 1) + epsilon
    denominator = variance + error_var
    post_mean = (center * error_var + obs_value * variance) / denominator
    shrink = jnp.sqrt(error_var / denominator)
    increment = post_mean + shrink * anomaly - prior_obs
    return (anomaly, variance, increment, jnp.stack([center, jnp.sqrt(variance)]))

def tapers(lat_pos, lon_pos, lat_cells, lon_cells, lon_total, lat_dev, lon_dev):
    lat_gap = (lat_cells[:, None] - lat_pos[None, :]) / lat_dev
    lon_gap = jnp.abs(lon_cells[:, None] - lon_pos[None, :])
    lon_gap = jnp.minimum(lon_gap, lon_total - lon_gap) / (0.5 * lon_dev)
    return (jnp.exp(-0.5 * lat_gap * lat_gap), jnp.exp(-0.5 * lon_gap * lon_gap))

def regress(current, mask_block, taper_lat, taper_lon, anomaly, variance, increment):
    mask_full = jnp.repeat(mask_block.astype(taper_lat.dtype), CLON, axis=-1)
    slabs = jnp.moveaxis(current.reshape(M, VARS * LEVELS, NLAT, NLON), 1, 0)
    masks = mask_full.reshape(VARS * LEVELS, NLAT, NLON)

    def update_slice(pair):
        level_slab, slab_mask = pair
        deviation = level_slab - lax.optimization_barrier(jnp.mean(level_slab, axis=0))
        covariance = jnp.einsum('mao,mj->aoj', deviation, anomaly, precision=lax.Precision.HIGHEST) / (M - 1)
        locality = slab_mask[:, :, None] * taper_lat[:, None, :] * taper_lon[None, :, :]
        return level_slab + jnp.einsum('aoj,mj->mao', locality * covariance / variance, increment, precision=lax.Precision.HIGHEST)
    updated = lax.map(update_slice, (slabs, masks))
    return jnp.moveaxis(updated, 0, 1).reshape(current.shape)

def blocks_of(source):
    shaped = source.reshape(source.shape[:-1] + (BLOCKS, OBLK))
    return jnp.moveaxis(shaped, -2, 0)

def reference(ensemble, obs_values, obs_error_var, obs_lat, obs_lon, obs_level, obs_frac, loc_mask):
    lat_cells = jnp.arange(NLAT).astype(ensemble.dtype)
    lon_cells = jnp.arange(NLON).astype(ensemble.dtype)
    current = ensemble
    prior_parts = []
    post_parts = []
    for batch_number in range(BATCHES):
        inputs = (blocks_of(obs_lat[batch_number]), blocks_of(obs_lon[batch_number]), blocks_of(obs_level[batch_number]), blocks_of(obs_frac[batch_number]), blocks_of(obs_values[batch_number]), blocks_of(obs_error_var[batch_number]), loc_mask[batch_number])

        def advance(analysis, block_data):
            lat_rows, lon_cols, level_ids, fraction, obs_value, error_var, mask_block = block_data
            prior_obs = forward(analysis.reshape(M, -1), lat_rows, lon_cols, level_ids, fraction)
            anomaly, variance, increment, summary_block = adjust(prior_obs, obs_value, error_var)
            taper_lat, taper_lon = tapers(lat_rows.astype(fraction.dtype) + fraction[0], lon_cols.astype(fraction.dtype) + fraction[1], lat_cells, lon_cells, NLON, CLAT, CLON)
            return (regress(analysis, mask_block, taper_lat, taper_lon, anomaly, variance, increment), summary_block)
        current, summaries = lax.scan(advance, current, inputs)
        prior_parts.append(jnp.moveaxis(summaries, 0, 1).reshape(2, NOBS))
        posterior = forward(current.reshape(M, -1), obs_lat[batch_number], obs_lon[batch_number], obs_level[batch_number], obs_frac[batch_number])
        post_parts.append(spread_stats(posterior))
    return (current, jnp.stack(prior_parts), jnp.stack(post_parts))
```

```python
import functools

import jax
import jax.numpy as jnp
from jax import lax
from jax.experimental import pallas as pl
from jax.experimental.pallas import tpu as pltpu
from jax.sharding import PartitionSpec as P

epsilon = 1e-06
AXES = ("lat", "lon", "lev")
LANES = 128
CHUNK = 4
f32, bf16, i32 = jnp.float32, jnp.bfloat16, jnp.int32


def split(values):
    high = values.astype(bf16)
    return high, (values - high.astype(f32)).astype(bf16)


def pick_kernel(nxt_ref, idx_ref, x_ref, e_ref):
    members = x_ref.shape[1]
    obs_total = idx_ref.shape[1]
    lane = lax.broadcasted_iota(i32, (members, LANES), 1)
    e_ref[...] = jnp.zeros_like(e_ref)

    def step(i):
        block, column = i // LANES, i % LANES
        for corner in range(4):
            cell = idx_ref[corner, i]
            held = cell >= 0
            safe = jnp.maximum(cell, 0)
            tile = x_ref[safe // LANES]
            turned = pltpu.roll(tile, (column - safe % LANES + LANES) % LANES, 1)
            put = (lane == column) & held
            e_ref[block, corner] = jnp.where(put, turned, e_ref[block, corner])
        return nxt_ref[i + 1]

    lax.while_loop(lambda i: i < obs_total, step, nxt_ref[0])


def batch_kernel(dims, where_ref, count_ref, list_ref, obs_ref, word_ref, x_ref, e_in, out_ref, prior_ref, post_ref,
                 xs, e_ref, loc_ref, lhs1_ref, lhs2_ref, pos_ref):
    lat_dev, lon_dev, lon_total = dims
    slabs, members = x_ref.shape[0], x_ref.shape[1]
    blocks = e_in.shape[0]
    lat_start, lon_start, keep = where_ref[0], where_ref[1], where_ref[2]
    xs[0:slabs] = x_ref[...]
    xs[slabs] = jnp.zeros((members, LANES), f32)
    e_ref[...] = e_in[...]
    pad_rows = 256 - 3 * members
    lat_scale = 1.0 / lat_dev
    lon_scale = 1.0 / (0.5 * lon_dev)

    def observe(block):
        row = obs_ref[block]
        p, q = row[2:3], row[3:4]
        result = (1.0 - p) * (1.0 - q) * e_ref[block, 0]
        result = result + p * (1.0 - q) * e_ref[block, 1]
        result = result + (1.0 - p) * q * e_ref[block, 2]
        result = result + p * q * e_ref[block, 3]
        center = jnp.sum(result, axis=0, keepdims=True) / members
        anomaly = result - center
        variance = jnp.sum(anomaly * anomaly, axis=0, keepdims=True) / (members - 1) + epsilon
        return row, result, center, anomaly, variance

    def lat_taper(rows, at):
        gap = (rows - at) * lat_scale
        return jnp.exp(-0.5 * gap * gap)

    def lon_taper(columns, at):
        gap = jnp.abs(columns - at)
        gap = jnp.minimum(gap, lon_total - gap) * lon_scale
        return jnp.exp(-0.5 * gap * gap)

    def update(tiles, locality):
        pad = jnp.zeros((pad_rows, LANES), bf16)
        columns = []
        for tile in tiles:
            high, low = split(tile)
            columns.append(jnp.concatenate([high, high, low, pad], axis=0))
        cov = jnp.dot(lhs1_ref[...], jnp.concatenate(columns, axis=1), preferred_element_type=f32)
        columns = []
        for number in range(len(tiles)):
            gain = cov[:, number * LANES:(number + 1) * LANES] * locality(number)
            columns.append(jnp.concatenate(split(gain), axis=0))
        moved = jnp.dot(lhs2_ref[...], jnp.concatenate(columns, axis=1), preferred_element_type=f32)
        return [
            tile + (moved[:members, number * LANES:(number + 1) * LANES] + moved[members:, number * LANES:(number + 1) * LANES])
            for number, tile in enumerate(tiles)
        ]

    def assimilate(block, carry):
        row, result, center, anomaly, variance = observe(block)
        y, r = row[4:5], row[5:6]
        denominator = variance + r
        post_mean = (center * r + y * variance) / denominator
        increment = post_mean + jnp.sqrt(r / denominator) * anomaly - result
        prior_ref[block] = jnp.concatenate([center, jnp.sqrt(variance)], axis=0)
        scaled = increment / (variance * (members - 1))
        r_high, r_low = split(scaled)
        lhs2_ref[...] = jnp.concatenate(
            [
                jnp.concatenate([r_high, r_high], axis=1),
                jnp.concatenate([r_low, jnp.zeros_like(r_low)], axis=1),
            ],
            axis=0,
        )
        d_high = anomaly.astype(bf16).astype(f32)
        d_low = anomaly - d_high
        packed = jnp.concatenate([d_high, d_low, d_high, jnp.zeros((pad_rows, LANES), f32)], axis=0)
        lhs1_ref[...] = packed.T.astype(bf16)
        lat_at = jnp.broadcast_to(row[0:1] + row[2:3], (LANES, LANES)).T
        lon_at = jnp.broadcast_to(row[1:2] + row[3:4], (LANES, LANES)).T
        pos_ref[0] = lat_at
        pos_ref[1] = lon_at
        columns = lon_start + lax.broadcasted_iota(i32, (LANES, LANES), 1)
        own_lon = lon_taper(columns.astype(f32), lon_at)
        for a in range(lat_dev):
            loc_ref[a] = lat_taper((lat_start + a).astype(f32), lat_at) * own_lon

        def stencil(step, c):
            later = block + 1 + step
            other = jnp.where(later < blocks, later, keep)
            orow = obs_ref[other]
            la, lo = pos_ref[0], pos_ref[1]
            lats = [lat_taper(orow[0:1], la), lat_taper(orow[0:1] + 1.0, la)]
            lons = [lon_taper(orow[1:2], lo), lon_taper(orow[6:7], lo)]

            def locality(corner):
                bit = ((word_ref[other, corner:corner + 1] >> block) & 1).astype(f32)
                return lats[corner % 2] * lons[corner // 2] * bit

            new = update([e_ref[other, corner] for corner in range(4)], locality)
            for corner in range(4):
                e_ref[other, corner] = new[corner]
            return c

        lax.fori_loop(0, blocks - 1 - block + (keep <= block).astype(i32), stencil, 0)

        def own(step, c):
            which = [list_ref[block, step * CHUNK + number] for number in range(CHUNK)]
            new = update([xs[w] for w in which], lambda number: loc_ref[which[number] % lat_dev])
            for number in range(CHUNK):
                xs[which[number]] = new[number]
            return c

        lax.fori_loop(0, pl.cdiv(count_ref[block], CHUNK), own, 0)
        return carry

    lax.fori_loop(0, blocks, assimilate, 0)
    out_ref[...] = xs[0:slabs]
    row, result, center, anomaly, variance = observe(keep)
    post_ref[...] = jnp.concatenate([center, jnp.sqrt(variance)], axis=0)


def word_kernel(slot_ref, table_ref, out_ref):
    slot = slot_ref[...]
    place = slot % LANES
    row = slot // LANES
    result = jnp.zeros_like(slot)
    for number in range(table_ref.shape[0]):
        line = jnp.broadcast_to(table_ref[number:number + 1], slot.shape)
        found = jnp.take_along_axis(line, place, axis=1)
        result = jnp.where(row == number, found, result)
    out_ref[...] = result


def body(ensemble, obs_values, obs_error_var, obs_lat, obs_lon, obs_level, obs_frac, loc_mask):
    members, var_count, level_dev, lat_dev, lon_dev = ensemble.shape
    batches, blocks = loc_mask.shape[:2]
    obs_total = obs_values.shape[1]
    lat_parts, lon_parts, lev_parts = (lax.axis_size(name) for name in AXES)
    lat_at, lon_at, lev_at = (lax.axis_index(name) for name in AXES)
    lon_total, level_total, lat_total = lon_dev * lon_parts, level_dev * lev_parts, lat_dev * lat_parts
    lat_start, lon_start, level_start = lat_at * lat_dev, lon_at * lon_dev, lev_at * level_dev
    slabs = var_count * level_dev * lat_dev
    keep = ((lat_at * lon_parts + lon_at) * lev_parts + lev_at) % blocks

    variable, level = obs_level // level_total, obs_level % level_total
    level_local = level - level_start
    cells, slots = [], []
    for row_step, col_step in ((0, 0), (1, 0), (0, 1), (1, 1)):
        row = obs_lat + row_step
        col = (obs_lon + col_step) % lon_total
        row_local, col_local = row - lat_start, col - lon_start
        held = (
            (level_local >= 0) & (level_local < level_dev) & (row_local >= 0) & (row_local < lat_dev)
            & (col_local >= 0) & (col_local < lon_dev)
        )
        cell = ((variable * level_dev + level_local) * lat_dev + row_local) * lon_dev + col_local
        cells.append(jnp.where(held, cell, -1))
        slots.append((obs_level * lat_total + row) * lon_parts + col // lon_dev)
    cells = jnp.stack(cells, axis=1)
    slots = jnp.stack(slots, axis=1)
    spots = jnp.where(jnp.max(cells, axis=1) >= 0, jnp.arange(obs_total, dtype=i32), obs_total)
    nxt = lax.cummin(spots, axis=1, reverse=True)
    nxt = jnp.concatenate([nxt, jnp.full((batches, 1), obs_total, i32)], axis=1)

    masks = lax.all_gather(loc_mask, AXES)
    masks = masks.reshape((lat_parts, lon_parts, lev_parts) + loc_mask.shape[:-1])
    bits = jnp.sum(masks << jnp.arange(blocks, dtype=i32)[:, None, None, None], axis=4)
    bits = bits.transpose(3, 4, 2, 5, 0, 6, 1).reshape(batches, -1)
    bits = jnp.pad(bits, ((0, 0), (0, -bits.shape[1] % LANES))).reshape(batches, -1, LANES)

    own = loc_mask.reshape(batches, blocks, slabs)
    count = jnp.sum(own, axis=2)
    rank = jnp.cumsum(own, axis=2) - 1
    padded = slabs + CHUNK
    hit = (rank[..., None] == jnp.arange(padded)) & (own[..., None] > 0)
    number = jnp.arange(slabs, dtype=i32)[:, None]
    active = slabs + jnp.sum(jnp.where(hit, number - slabs, 0), axis=2)

    def rows_of(values):
        return values.astype(f32).reshape(batches, blocks, LANES)

    obs_rows = jnp.stack(
        [rows_of(v) for v in (obs_lat, obs_lon, obs_frac[:, 0], obs_frac[:, 1], obs_values, obs_error_var,
                              (obs_lon + 1) % lon_total, obs_lat)],
        axis=2,
    )
    where = jnp.stack([lat_start, lon_start, keep]).astype(i32)
    smem = pl.BlockSpec(memory_space=pltpu.SMEM)
    vmem = pl.BlockSpec(memory_space=pltpu.VMEM)
    params = pltpu.CompilerParams(vmem_limit_bytes=56 * 1024 * 1024)
    words = pl.pallas_call(
        word_kernel,
        out_shape=jax.ShapeDtypeStruct((4 * obs_total // LANES, LANES), i32),
        in_specs=[vmem, vmem],
        out_specs=vmem,
    )
    pick = pl.pallas_call(
        pick_kernel,
        out_shape=jax.ShapeDtypeStruct((blocks, 4, members, LANES), f32),
        in_specs=[smem, smem, vmem],
        out_specs=vmem,
        compiler_params=params,
    )
    assimilate = pl.pallas_call(
        functools.partial(batch_kernel, (lat_dev, lon_dev, lon_total)),
        out_shape=(
            jax.ShapeDtypeStruct((slabs, members, LANES), f32),
            jax.ShapeDtypeStruct((blocks, 2, LANES), f32),
            jax.ShapeDtypeStruct((2, LANES), f32),
        ),
        in_specs=[smem, smem, smem, vmem, vmem, vmem, vmem],
        out_specs=(vmem, vmem, vmem),
        scratch_shapes=[
            pltpu.VMEM((slabs + 1, members, LANES), f32),
            pltpu.VMEM((blocks, 4, members, LANES), f32),
            pltpu.VMEM((lat_dev, LANES, LANES), f32),
            pltpu.VMEM((LANES, 256), bf16),
            pltpu.VMEM((2 * members, 256), bf16),
            pltpu.VMEM((2, LANES, LANES), f32),
        ],
        compiler_params=params,
    )
    x = ensemble.reshape(members, slabs, LANES).transpose(1, 0, 2)
    prior_parts, post_parts = [], []
    for batch in range(batches):
        word = words(slots[batch].reshape(-1, LANES), bits[batch])
        word = word.reshape(4, blocks, LANES).transpose(1, 0, 2)
        stencils = lax.psum(pick(nxt[batch], cells[batch], x), AXES)
        x, prior, post = assimilate(where, count[batch], active[batch], obs_rows[batch], word, x, stencils)
        prior_parts.append(prior.transpose(1, 0, 2).reshape(2, obs_total))
        post_parts.append(post)
    posts = lax.all_gather(jnp.stack(post_parts), AXES)[:blocks]
    posts = posts.transpose(1, 2, 0, 3).reshape(batches, 2, obs_total)
    analysis = x.transpose(1, 0, 2).reshape(ensemble.shape)
    return analysis, jnp.stack(prior_parts), posts


def solution(mesh):
    state = P(None, None, "lev", "lat", "lon")
    return jax.shard_map(
        body,
        mesh=mesh,
        in_specs=(state, P(), P(), P(), P(), P(), P(), P(None, None, None, "lev", "lat", "lon")),
        out_specs=(state, P(), P()),
        check_vma=False,
    )
```

```python
import functools

import jax
import jax.numpy as jnp
from jax import lax
from jax.experimental import pallas as pl
from jax.experimental.pallas import tpu as pltpu
from jax.sharding import PartitionSpec as P

epsilon = 1e-06
AXES = ("lat", "lon", "lev")
LANES = 128
CHUNK = 20
GROUP = 3
f32, bf16, i32 = jnp.float32, jnp.bfloat16, jnp.int32


def split(values):
    high = values.astype(bf16)
    return high, (values - high.astype(f32)).astype(bf16)


def shifted(values, name, by):
    size = lax.axis_size(name)
    return lax.ppermute(values, name, [(i, (i + by) % size) for i in range(size)])


def share_sum(values, name):
    size, me = lax.axis_size(name), lax.axis_index(name)
    parts = values.reshape((size, values.shape[0] // size) + values.shape[1:])
    total = lax.dynamic_index_in_dim(parts, me, 0, False)
    for by in range(1, size):
        total = total + shifted(lax.dynamic_index_in_dim(parts, (me + by) % size, 0, False), name, by)
    return total


def collect(values, name):
    size, me = lax.axis_size(name), lax.axis_index(name)
    result = jnp.zeros((size,) + values.shape, values.dtype)
    result = lax.dynamic_update_index_in_dim(result, values, me, 0)
    for by in range(1, size):
        result = lax.dynamic_update_index_in_dim(result, shifted(values, name, by), (me - by) % size, 0)
    return result


def collect_all(values):
    for name in ("lon", "lat", "lev"):
        values = collect(values, name)
    return values


def total_of(values):
    rows = values.reshape(-1, LANES)
    for name in ("lev", "lat", "lon"):
        rows = share_sum(rows, name)
    for name in ("lon", "lat", "lev"):
        rows = collect(rows, name).reshape(-1, LANES)
    return rows.reshape(values.shape)


def pick_kernel(nxt_ref, idx_ref, x_ref, e_ref):
    members = x_ref.shape[1]
    obs_total = idx_ref.shape[1]
    lane = lax.broadcasted_iota(i32, (members, LANES), 1)
    e_ref[...] = jnp.zeros_like(e_ref)

    def step(i):
        block, column = i // LANES, i % LANES
        for corner in range(4):
            cell = idx_ref[corner, i]
            held = cell >= 0
            safe = jnp.maximum(cell, 0)
            tile = x_ref[safe // LANES]
            turned = pltpu.roll(tile, (column - safe % LANES + LANES) % LANES, 1)
            put = (lane == column) & held
            e_ref[block, corner] = jnp.where(put, turned, e_ref[block, corner])
        return nxt_ref[i + 1]

    lax.while_loop(lambda i: i < obs_total, step, nxt_ref[0])


def batch_kernel(dims, where_ref, count_ref, list_ref, obs_ref, word_ref, x_ref, e_in, out_ref, prior_ref, post_ref,
                 xs, e_ref, loc_ref, lhs1_ref, lhs2_ref, pos_ref):
    lat_dev, lon_dev, lon_total = dims
    slabs, members = x_ref.shape[0], x_ref.shape[1]
    blocks = e_in.shape[0]
    lat_start, lon_start, keep = where_ref[0], where_ref[1], where_ref[2]
    xs[0:slabs] = x_ref[...]
    xs[slabs] = jnp.zeros((members, LANES), f32)
    e_ref[0:blocks] = e_in[...]
    e_ref[blocks] = jnp.zeros((4, members, LANES), f32)
    pad_rows = 256 - 3 * members
    lat_scale = 1.0 / lat_dev
    lon_scale = 1.0 / (0.5 * lon_dev)

    def observe(block):
        row = obs_ref[block]
        p, q = row[2:3], row[3:4]
        result = (1.0 - p) * (1.0 - q) * e_ref[block, 0]
        result = result + p * (1.0 - q) * e_ref[block, 1]
        result = result + (1.0 - p) * q * e_ref[block, 2]
        result = result + p * q * e_ref[block, 3]
        center = jnp.sum(result, axis=0, keepdims=True) / members
        anomaly = result - center
        variance = jnp.sum(anomaly * anomaly, axis=0, keepdims=True) / (members - 1) + epsilon
        return row, result, center, anomaly, variance

    def lat_taper(rows, at):
        gap = (rows - at) * lat_scale
        return jnp.exp(-0.5 * gap * gap)

    def lon_taper(columns, at):
        gap = jnp.abs(columns - at)
        gap = jnp.minimum(gap, lon_total - gap) * lon_scale
        return jnp.exp(-0.5 * gap * gap)

    def update(tiles, locality):
        pad = jnp.zeros((pad_rows, LANES), bf16)
        columns = []
        for tile in tiles:
            high, low = split(tile)
            columns.append(jnp.concatenate([high, high, low, pad], axis=0))
        cov = jnp.dot(lhs1_ref[...], jnp.concatenate(columns, axis=1), preferred_element_type=f32)
        columns = []
        for number in range(len(tiles)):
            gain = cov[:, number * LANES:(number + 1) * LANES] * locality(number)
            columns.append(jnp.concatenate(split(gain), axis=0))
        moved = jnp.dot(lhs2_ref[...], jnp.concatenate(columns, axis=1), preferred_element_type=f32)
        return [
            tile + (moved[:members, number * LANES:(number + 1) * LANES] + moved[members:, number * LANES:(number + 1) * LANES])
            for number, tile in enumerate(tiles)
        ]

    def group_of(block, number):
        later = block + 1 + number
        last = jnp.where((later == blocks) & (keep <= block), keep, blocks)
        return jnp.where(later < blocks, later, last)

    def assimilate(block, carry):
        row, result, center, anomaly, variance = observe(block)
        y, r = row[4:5], row[5:6]
        denominator = variance + r
        post_mean = (center * r + y * variance) / denominator
        increment = post_mean + jnp.sqrt(r / denominator) * anomaly - result
        prior_ref[block] = jnp.concatenate([center, jnp.sqrt(variance)], axis=0)
        scaled = increment / (variance * (members - 1))
        r_high, r_low = split(scaled)
        lhs2_ref[...] = jnp.concatenate(
            [
                jnp.concatenate([r_high, r_high], axis=1),
                jnp.concatenate([r_low, jnp.zeros_like(r_low)], axis=1),
            ],
            axis=0,
        )
        d_high = anomaly.astype(bf16).astype(f32)
        d_low = anomaly - d_high
        packed = jnp.concatenate([d_high, d_low, d_high, jnp.zeros((pad_rows, LANES), f32)], axis=0)
        lhs1_ref[...] = packed.T.astype(bf16)
        lat_at = jnp.broadcast_to(row[0:1] + row[2:3], (LANES, LANES)).T
        lon_at = jnp.broadcast_to(row[1:2] + row[3:4], (LANES, LANES)).T
        pos_ref[0] = lat_at
        pos_ref[1] = lon_at
        columns = lon_start + lax.broadcasted_iota(i32, (LANES, LANES), 1)
        own_lon = lon_taper(columns.astype(f32), lon_at)
        for a in range(lat_dev):
            loc_ref[a] = lat_taper((lat_start + a).astype(f32), lat_at) * own_lon

        def stencil(step, c):
            others = [group_of(block, step * GROUP + number) for number in range(GROUP)]
            la, lo = pos_ref[0], pos_ref[1]
            lats, lons, bits = [], [], []
            for other in others:
                orow = obs_ref[jnp.minimum(other, blocks - 1)]
                lats.append([lat_taper(orow[0:1], la), lat_taper(orow[0:1] + 1.0, la)])
                lons.append([lon_taper(orow[1:2], lo), lon_taper(orow[6:7], lo)])
                bits.append(((word_ref[jnp.minimum(other, blocks - 1)] >> block) & 1).astype(f32))

            def locality(number):
                which, corner = number // 4, number % 4
                return lats[which][corner % 2] * lons[which][corner // 2] * bits[which][corner:corner + 1]

            new = update([e_ref[other, corner] for other in others for corner in range(4)], locality)
            for number, tile in enumerate(new):
                e_ref[others[number // 4], number % 4] = tile
            return c

        pending = blocks - 1 - block + (keep <= block).astype(i32)
        lax.fori_loop(0, pl.cdiv(pending, GROUP), stencil, 0)

        def own(step, c):
            which = [list_ref[block, step * CHUNK + number] for number in range(CHUNK)]
            new = update([xs[w] for w in which], lambda number: loc_ref[which[number] % lat_dev])
            for number in range(CHUNK):
                xs[which[number]] = new[number]
            return c

        lax.fori_loop(0, pl.cdiv(count_ref[block], CHUNK), own, 0)
        return carry

    lax.fori_loop(0, blocks, assimilate, 0)
    out_ref[...] = xs[0:slabs]
    row, result, center, anomaly, variance = observe(keep)
    post_ref[...] = jnp.concatenate([center, jnp.sqrt(variance)], axis=0)


def word_kernel(slot_ref, table_ref, out_ref):
    slot = slot_ref[...]
    place = slot % LANES
    row = slot // LANES
    result = jnp.zeros_like(slot)
    for number in range(table_ref.shape[0]):
        line = jnp.broadcast_to(table_ref[number:number + 1], slot.shape)
        found = jnp.take_along_axis(line, place, axis=1)
        result = jnp.where(row == number, found, result)
    out_ref[...] = result


def body(ensemble, obs_values, obs_error_var, obs_lat, obs_lon, obs_level, obs_frac, loc_mask):
    members, var_count, level_dev, lat_dev, lon_dev = ensemble.shape
    batches, blocks = loc_mask.shape[:2]
    obs_total = obs_values.shape[1]
    lat_parts, lon_parts, lev_parts = (lax.axis_size(name) for name in AXES)
    lat_at, lon_at, lev_at = (lax.axis_index(name) for name in AXES)
    lon_total, level_total, lat_total = lon_dev * lon_parts, level_dev * lev_parts, lat_dev * lat_parts
    lat_start, lon_start, level_start = lat_at * lat_dev, lon_at * lon_dev, lev_at * level_dev
    slabs = var_count * level_dev * lat_dev
    keep = (lat_at * lon_parts + lon_at) % blocks

    variable, level = obs_level // level_total, obs_level % level_total
    level_local = level - level_start
    cells, slots = [], []
    for row_step, col_step in ((0, 0), (1, 0), (0, 1), (1, 1)):
        row = obs_lat + row_step
        col = (obs_lon + col_step) % lon_total
        row_local, col_local = row - lat_start, col - lon_start
        held = (
            (level_local >= 0) & (level_local < level_dev) & (row_local >= 0) & (row_local < lat_dev)
            & (col_local >= 0) & (col_local < lon_dev)
        )
        cell = ((variable * level_dev + level_local) * lat_dev + row_local) * lon_dev + col_local
        cells.append(jnp.where(held, cell, -1))
        slots.append((obs_level * lat_total + row) * lon_parts + col // lon_dev)
    cells = jnp.stack(cells, axis=1)
    slots = jnp.stack(slots, axis=1)
    spots = jnp.where(jnp.max(cells, axis=1) >= 0, jnp.arange(obs_total, dtype=i32), obs_total)
    nxt = lax.cummin(spots, axis=1, reverse=True)
    nxt = jnp.concatenate([nxt, jnp.full((batches, 1), obs_total, i32)], axis=1)

    masks = collect_all(loc_mask.reshape(batches * blocks, slabs))
    masks = masks.reshape((lev_parts, lat_parts, lon_parts) + loc_mask.shape[:-1])
    bits = jnp.sum(masks << jnp.arange(blocks, dtype=i32)[:, None, None, None], axis=4)
    bits = bits.transpose(3, 4, 0, 5, 1, 6, 2).reshape(batches, -1)
    bits = jnp.pad(bits, ((0, 0), (0, -bits.shape[1] % LANES))).reshape(batches, -1, LANES)

    own = loc_mask.reshape(batches, blocks, slabs)
    count = jnp.sum(own, axis=2)
    rank = jnp.cumsum(own, axis=2) - 1
    padded = slabs + CHUNK
    hit = (rank[..., None] == jnp.arange(padded)) & (own[..., None] > 0)
    number = jnp.arange(slabs, dtype=i32)[:, None]
    active = slabs + jnp.sum(jnp.where(hit, number - slabs, 0), axis=2)

    def rows_of(values):
        return values.astype(f32).reshape(batches, blocks, LANES)

    obs_rows = jnp.stack(
        [rows_of(v) for v in (obs_lat, obs_lon, obs_frac[:, 0], obs_frac[:, 1], obs_values, obs_error_var,
                              (obs_lon + 1) % lon_total, obs_lat)],
        axis=2,
    )
    where = jnp.stack([lat_start, lon_start, keep]).astype(i32)
    smem = pl.BlockSpec(memory_space=pltpu.SMEM)
    vmem = pl.BlockSpec(memory_space=pltpu.VMEM)
    params = pltpu.CompilerParams(vmem_limit_bytes=56 * 1024 * 1024)
    words = pl.pallas_call(
        word_kernel,
        out_shape=jax.ShapeDtypeStruct((4 * obs_total // LANES, LANES), i32),
        in_specs=[vmem, vmem],
        out_specs=vmem,
    )
    pick = pl.pallas_call(
        pick_kernel,
        out_shape=jax.ShapeDtypeStruct((blocks, 4, members, LANES), f32),
        in_specs=[smem, smem, vmem],
        out_specs=vmem,
        compiler_params=params,
    )
    assimilate = pl.pallas_call(
        functools.partial(batch_kernel, (lat_dev, lon_dev, lon_total)),
        out_shape=(
            jax.ShapeDtypeStruct((slabs, members, LANES), f32),
            jax.ShapeDtypeStruct((blocks, 2, LANES), f32),
            jax.ShapeDtypeStruct((2, LANES), f32),
        ),
        in_specs=[smem, smem, smem, vmem, vmem, vmem, vmem],
        out_specs=(vmem, vmem, vmem),
        scratch_shapes=[
            pltpu.VMEM((slabs + 1, members, LANES), f32),
            pltpu.VMEM((blocks + 1, 4, members, LANES), f32),
            pltpu.VMEM((lat_dev, LANES, LANES), f32),
            pltpu.VMEM((LANES, 256), bf16),
            pltpu.VMEM((2 * members, 256), bf16),
            pltpu.VMEM((2, LANES, LANES), f32),
        ],
        compiler_params=params,
    )
    x = ensemble.reshape(members, slabs, LANES).transpose(1, 0, 2)
    prior_parts, post_parts = [], []
    for batch in range(batches):
        word = words(slots[batch].reshape(-1, LANES), bits[batch])
        word = word.reshape(4, blocks, LANES).transpose(1, 0, 2)
        stencils = total_of(pick(nxt[batch], cells[batch], x))
        x, prior, post = assimilate(where, count[batch], active[batch], obs_rows[batch], word, x, stencils)
        prior_parts.append(prior.transpose(1, 0, 2).reshape(2, obs_total))
        post_parts.append(post)
    posts = collect(collect(jnp.concatenate(post_parts, axis=0), "lon"), "lat").reshape(-1, 2 * batches, LANES)
    posts = posts[:blocks].transpose(1, 0, 2).reshape(batches, 2, obs_total)
    analysis = x.transpose(1, 0, 2).reshape(ensemble.shape)
    return analysis, jnp.stack(prior_parts), posts


def solution(mesh):
    state = P(None, None, "lev", "lat", "lon")
    return jax.shard_map(
        body,
        mesh=mesh,
        in_specs=(state, P(), P(), P(), P(), P(), P(), P(None, None, None, "lev", "lat", "lon")),
        out_specs=(state, P(), P()),
        check_vma=False,
    )
```

```python
import functools

import jax
import jax.numpy as jnp
from jax import lax
from jax.experimental import pallas as pl
from jax.experimental.pallas import tpu as pltpu
from jax.sharding import PartitionSpec as P

epsilon = 1e-06
AXES = ("lat", "lon", "lev")
LANES = 128
CHUNK = 20
HALF_LOG2E = 0.7213475204444817
GROUP = 3
f32, bf16, i32 = jnp.float32, jnp.bfloat16, jnp.int32


def split(values):
    high = values.astype(bf16)
    return high, (values - high.astype(f32)).astype(bf16)


def shifted(values, name, by):
    size = lax.axis_size(name)
    return lax.ppermute(values, name, [(i, (i + by) % size) for i in range(size)])


def share_sum(values, name):
    size, me = lax.axis_size(name), lax.axis_index(name)
    parts = values.reshape((size, values.shape[0] // size) + values.shape[1:])
    total = lax.dynamic_index_in_dim(parts, me, 0, False)
    for by in range(1, size):
        total = total + shifted(lax.dynamic_index_in_dim(parts, (me + by) % size, 0, False), name, by)
    return total


def collect(values, name):
    size, me = lax.axis_size(name), lax.axis_index(name)
    result = jnp.zeros((size,) + values.shape, values.dtype)
    result = lax.dynamic_update_index_in_dim(result, values, me, 0)
    for by in range(1, size):
        result = lax.dynamic_update_index_in_dim(result, shifted(values, name, by), (me - by) % size, 0)
    return result


def collect_all(values):
    for name in ("lon", "lat", "lev"):
        values = collect(values, name)
    return values


def total_of(values):
    rows = values.reshape(-1, LANES)
    for name in ("lev", "lat", "lon"):
        rows = share_sum(rows, name)
    for name in ("lon", "lat", "lev"):
        rows = collect(rows, name).reshape(-1, LANES)
    return rows.reshape(values.shape)


def pick_kernel(nxt_ref, idx_ref, x_ref, e_ref):
    members = x_ref.shape[1]
    obs_total = idx_ref.shape[1]
    lane = lax.broadcasted_iota(i32, (members, LANES), 1)
    e_ref[...] = jnp.zeros_like(e_ref)

    def step(i):
        block, column = i // LANES, i % LANES
        for corner in range(4):
            cell = idx_ref[corner, i]
            held = cell >= 0
            safe = jnp.maximum(cell, 0)
            tile = x_ref[safe // LANES]
            turned = pltpu.roll(tile, (column - safe % LANES + LANES) % LANES, 1)
            put = (lane == column) & held
            e_ref[block, corner] = jnp.where(put, turned, e_ref[block, corner])
        return nxt_ref[i + 1]

    lax.while_loop(lambda i: i < obs_total, step, nxt_ref[0])


def batch_kernel(dims, where_ref, count_ref, list_ref, obs_ref, word_ref, x_ref, e_in, out_ref, prior_ref, post_ref,
                 xs, e_ref, loc_ref, lhs1_ref, lhs2_ref, pos_ref):
    lat_dev, lon_dev, lon_total = dims
    slabs, members = x_ref.shape[0], x_ref.shape[1]
    blocks = e_in.shape[0]
    lat_start, lon_start, keep = where_ref[0], where_ref[1], where_ref[2]
    xs[0:slabs] = x_ref[...]
    xs[slabs] = jnp.zeros((members, LANES), f32)
    e_ref[0:blocks] = e_in[...]
    e_ref[blocks] = jnp.zeros((4, members, LANES), f32)
    pad_rows = 256 - 3 * members
    lat_scale = HALF_LOG2E**0.5 / lat_dev
    lon_scale = HALF_LOG2E**0.5 / (0.5 * lon_dev)

    def observe(block):
        row = obs_ref[block]
        p, q = row[2:3], row[3:4]
        result = (1.0 - p) * (1.0 - q) * e_ref[block, 0]
        result = result + p * (1.0 - q) * e_ref[block, 1]
        result = result + (1.0 - p) * q * e_ref[block, 2]
        result = result + p * q * e_ref[block, 3]
        center = jnp.sum(result, axis=0, keepdims=True) / members
        anomaly = result - center
        variance = jnp.sum(anomaly * anomaly, axis=0, keepdims=True) / (members - 1) + epsilon
        return row, result, center, anomaly, variance

    def lat_taper(rows, at):
        gap = rows * lat_scale - at
        return jnp.exp2(-(gap * gap))

    def lon_taper(columns, at):
        gap = jnp.abs(columns * lon_scale - at)
        gap = jnp.minimum(gap, lon_total * lon_scale - gap)
        return jnp.exp2(-(gap * gap))

    def update(tiles, locality, bit=None):
        pad = jnp.zeros((pad_rows, LANES), bf16)
        columns = []
        for tile in tiles:
            high, low = split(tile)
            columns.append(jnp.concatenate([high, high, low, pad], axis=0))
        cov = jnp.dot(lhs1_ref[...], jnp.concatenate(columns, axis=1), preferred_element_type=f32)
        columns = []
        for number in range(len(tiles)):
            gain = cov[:, number * LANES:(number + 1) * LANES] * locality(number)
            columns.append(jnp.concatenate(split(gain), axis=0))
        moved = jnp.dot(lhs2_ref[...], jnp.concatenate(columns, axis=1), preferred_element_type=f32)
        results = []
        for number, tile in enumerate(tiles):
            lanes = slice(number * LANES, (number + 1) * LANES)
            change = moved[:members, lanes] + moved[members:, lanes]
            results.append(tile + (change if bit is None else change * bit(number)))
        return results

    def group_of(block, number):
        later = block + 1 + number
        last = jnp.where((later == blocks) & (keep <= block), keep, blocks)
        return jnp.where(later < blocks, later, last)

    def assimilate(block, carry):
        row, result, center, anomaly, variance = observe(block)
        y, r = row[4:5], row[5:6]
        denominator = variance + r
        post_mean = (center * r + y * variance) / denominator
        increment = post_mean + jnp.sqrt(r / denominator) * anomaly - result
        prior_ref[block] = jnp.concatenate([center, jnp.sqrt(variance)], axis=0)
        scaled = increment / (variance * (members - 1))
        r_high, r_low = split(scaled)
        lhs2_ref[...] = jnp.concatenate(
            [
                jnp.concatenate([r_high, r_high], axis=1),
                jnp.concatenate([r_low, jnp.zeros_like(r_low)], axis=1),
            ],
            axis=0,
        )
        d_high = anomaly.astype(bf16).astype(f32)
        d_low = anomaly - d_high
        packed = jnp.concatenate([d_high, d_low, d_high, jnp.zeros((pad_rows, LANES), f32)], axis=0)
        lhs1_ref[...] = packed.T.astype(bf16)
        lat_at = jnp.broadcast_to((row[0:1] + row[2:3]) * lat_scale, (LANES, LANES)).T
        lon_at = jnp.broadcast_to((row[1:2] + row[3:4]) * lon_scale, (LANES, LANES)).T
        pos_ref[0] = lat_at
        pos_ref[1] = lon_at
        columns = lon_start + lax.broadcasted_iota(i32, (LANES, LANES), 1)
        own_lon = lon_taper(columns.astype(f32), lon_at)
        for a in range(lat_dev):
            loc_ref[a] = lat_taper((lat_start + a).astype(f32), lat_at) * own_lon

        def stencil(step, c):
            others = [group_of(block, step * GROUP + number) for number in range(GROUP)]
            la, lo = pos_ref[0], pos_ref[1]
            lats, lons, bits = [], [], []
            for other in others:
                orow = obs_ref[jnp.minimum(other, blocks - 1)]
                lats.append([lat_taper(orow[0:1], la), lat_taper(orow[0:1] + 1.0, la)])
                lons.append([lon_taper(orow[1:2], lo), lon_taper(orow[6:7], lo)])
                bits.append(((word_ref[jnp.minimum(other, blocks - 1)] >> block) & 1).astype(f32))

            def locality(number):
                which, corner = number // 4, number % 4
                return lats[which][corner % 2] * lons[which][corner // 2]

            def bit(number):
                return bits[number // 4][number % 4:number % 4 + 1]

            new = update([e_ref[other, corner] for other in others for corner in range(4)], locality, bit)
            for number, tile in enumerate(new):
                e_ref[others[number // 4], number % 4] = tile
            return c

        pending = blocks - 1 - block + (keep <= block).astype(i32)
        lax.fori_loop(0, pl.cdiv(pending, GROUP), stencil, 0)

        def own(step, c):
            which = [list_ref[block, step * CHUNK + number] for number in range(CHUNK)]
            new = update([xs[w] for w in which], lambda number: loc_ref[which[number] % lat_dev])
            for number in range(CHUNK):
                xs[which[number]] = new[number]
            return c

        lax.fori_loop(0, pl.cdiv(count_ref[block], CHUNK), own, 0)
        return carry

    lax.fori_loop(0, blocks, assimilate, 0)
    out_ref[...] = xs[0:slabs]
    row, result, center, anomaly, variance = observe(keep)
    post_ref[...] = jnp.concatenate([center, jnp.sqrt(variance)], axis=0)


def word_kernel(slot_ref, table_ref, out_ref):
    for batch in range(slot_ref.shape[0]):
        slot = slot_ref[batch]
        place = slot % LANES
        row = slot // LANES
        result = jnp.zeros_like(slot)
        for number in range(table_ref.shape[1]):
            line = jnp.broadcast_to(table_ref[batch, number:number + 1], slot.shape)
            found = jnp.take_along_axis(line, place, axis=1)
            result = jnp.where(row == number, found, result)
        out_ref[batch] = result


def body(ensemble, obs_values, obs_error_var, obs_lat, obs_lon, obs_level, obs_frac, loc_mask):
    members, var_count, level_dev, lat_dev, lon_dev = ensemble.shape
    batches, blocks = loc_mask.shape[:2]
    obs_total = obs_values.shape[1]
    lat_parts, lon_parts, lev_parts = (lax.axis_size(name) for name in AXES)
    lat_at, lon_at, lev_at = (lax.axis_index(name) for name in AXES)
    lon_total, level_total, lat_total = lon_dev * lon_parts, level_dev * lev_parts, lat_dev * lat_parts
    lat_start, lon_start, level_start = lat_at * lat_dev, lon_at * lon_dev, lev_at * level_dev
    slabs = var_count * level_dev * lat_dev
    keep = (lat_at * lon_parts + lon_at) % blocks

    variable, level = obs_level // level_total, obs_level % level_total
    level_local = level - level_start
    cells, slots = [], []
    for row_step, col_step in ((0, 0), (1, 0), (0, 1), (1, 1)):
        row = obs_lat + row_step
        col = (obs_lon + col_step) % lon_total
        row_local, col_local = row - lat_start, col - lon_start
        held = (
            (level_local >= 0) & (level_local < level_dev) & (row_local >= 0) & (row_local < lat_dev)
            & (col_local >= 0) & (col_local < lon_dev)
        )
        cell = ((variable * level_dev + level_local) * lat_dev + row_local) * lon_dev + col_local
        cells.append(jnp.where(held, cell, -1))
        slots.append((obs_level * lat_total + row) * lon_parts + col // lon_dev)
    cells = jnp.stack(cells, axis=1)
    slots = jnp.stack([slot.reshape(batches, blocks, LANES) for slot in slots], axis=2)
    spots = jnp.where(jnp.max(cells, axis=1) >= 0, jnp.arange(obs_total, dtype=i32), obs_total)
    grid = spots.reshape(batches, blocks, LANES)
    lane = jnp.arange(LANES)
    inside = jnp.min(jnp.where(lane[:, None] <= lane, grid[:, :, None, :], obs_total), axis=3)
    number = jnp.arange(blocks)
    beyond = jnp.min(jnp.where(number[:, None] < number, jnp.min(grid, axis=2)[:, None, :], obs_total), axis=2)
    nxt = jnp.minimum(inside, beyond[:, :, None]).reshape(batches, obs_total)
    nxt = jnp.concatenate([nxt, jnp.full((batches, 1), obs_total, i32)], axis=1)

    masks = collect_all(loc_mask.reshape(batches * blocks, slabs))
    masks = masks.reshape(lev_parts, lat_parts, lon_parts, batches, blocks, slabs)
    bits = jnp.sum(masks << jnp.arange(blocks, dtype=i32)[:, None], axis=4)
    bits = lax.optimization_barrier(bits).reshape(lev_parts, lat_parts, lon_parts, batches, var_count, level_dev, lat_dev)
    bits = bits.transpose(3, 4, 0, 5, 1, 6, 2).reshape(batches, -1)
    bits = jnp.pad(bits, ((0, 0), (0, -bits.shape[1] % LANES))).reshape(batches, -1, LANES)

    own = loc_mask.reshape(batches, blocks, slabs)
    count = jnp.sum(own, axis=2)
    rank = jnp.cumsum(own, axis=2) - 1
    padded = slabs + CHUNK
    hit = (rank[..., None] == jnp.arange(padded)) & (own[..., None] > 0)
    number = jnp.arange(slabs, dtype=i32)[:, None]
    active = slabs + jnp.sum(jnp.where(hit, number - slabs, 0), axis=2)

    def rows_of(values):
        return values.astype(f32).reshape(batches, blocks, LANES)

    obs_rows = jnp.stack(
        [rows_of(v) for v in (obs_lat, obs_lon, obs_frac[:, 0], obs_frac[:, 1], obs_values, obs_error_var,
                              (obs_lon + 1) % lon_total, obs_lat)],
        axis=2,
    )
    where = jnp.stack([lat_start, lon_start, keep]).astype(i32)
    smem = pl.BlockSpec(memory_space=pltpu.SMEM)
    vmem = pl.BlockSpec(memory_space=pltpu.VMEM)
    params = pltpu.CompilerParams(vmem_limit_bytes=56 * 1024 * 1024)
    words = pl.pallas_call(
        word_kernel,
        out_shape=jax.ShapeDtypeStruct((batches, blocks * 4, LANES), i32),
        in_specs=[vmem, vmem],
        out_specs=vmem,
    )(slots.reshape(batches, -1, LANES), bits).reshape(batches, blocks, 4, LANES)
    pick = pl.pallas_call(
        pick_kernel,
        out_shape=jax.ShapeDtypeStruct((blocks, 4, members, LANES), f32),
        in_specs=[smem, smem, vmem],
        out_specs=vmem,
        compiler_params=params,
    )
    assimilate = pl.pallas_call(
        functools.partial(batch_kernel, (lat_dev, lon_dev, lon_total)),
        out_shape=(
            jax.ShapeDtypeStruct((slabs, members, LANES), f32),
            jax.ShapeDtypeStruct((blocks, 2, LANES), f32),
            jax.ShapeDtypeStruct((2, LANES), f32),
        ),
        in_specs=[smem, smem, smem, vmem, vmem, vmem, vmem],
        out_specs=(vmem, vmem, vmem),
        scratch_shapes=[
            pltpu.VMEM((slabs + 1, members, LANES), f32),
            pltpu.VMEM((blocks + 1, 4, members, LANES), f32),
            pltpu.VMEM((lat_dev, LANES, LANES), f32),
            pltpu.VMEM((LANES, 256), bf16),
            pltpu.VMEM((2 * members, 256), bf16),
            pltpu.VMEM((2, LANES, LANES), f32),
        ],
        compiler_params=params,
    )
    x = ensemble.reshape(members, slabs, LANES).transpose(1, 0, 2)
    prior_parts, post_parts = [], []
    for batch in range(batches):
        stencils = total_of(pick(nxt[batch], cells[batch], x))
        x, prior, post = assimilate(where, count[batch], active[batch], obs_rows[batch], words[batch], x, stencils)
        prior_parts.append(prior.transpose(1, 0, 2).reshape(2, obs_total))
        post_parts.append(post)
    posts = collect(collect(jnp.concatenate(post_parts, axis=0), "lon"), "lat").reshape(-1, 2 * batches, LANES)
    posts = posts[:blocks].transpose(1, 0, 2).reshape(batches, 2, obs_total)
    analysis = x.transpose(1, 0, 2).reshape(ensemble.shape)
    return analysis, jnp.stack(prior_parts), posts


def solution(mesh):
    state = P(None, None, "lev", "lat", "lon")
    return jax.shard_map(
        body,
        mesh=mesh,
        in_specs=(state, P(), P(), P(), P(), P(), P(), P(None, None, None, "lev", "lat", "lon")),
        out_specs=(state, P(), P()),
        check_vma=False,
    )
```

```python
import functools

import jax
import jax.numpy as jnp
from jax import lax
from jax.experimental import pallas as pl
from jax.experimental.pallas import tpu as pltpu
from jax.sharding import PartitionSpec as P

epsilon = 1e-06
AXES = ("lat", "lon", "lev")
LANES = 128
CHUNK = 20
HALF_LOG2E = 0.7213475204444817
GROUP = 3
f32, bf16, i32 = jnp.float32, jnp.bfloat16, jnp.int32


def split(values):
    high = values.astype(bf16)
    return high, (values - high.astype(f32)).astype(bf16)


def shifted(values, name, by):
    size = lax.axis_size(name)
    return lax.ppermute(values, name, [(i, (i + by) % size) for i in range(size)])


def share_sum(values, name):
    size, me = lax.axis_size(name), lax.axis_index(name)
    parts = values.reshape(values.shape[0], size, -1, LANES)
    total = lax.dynamic_index_in_dim(parts, me, 1, False)
    for by in range(1, size):
        total = total + shifted(lax.dynamic_index_in_dim(parts, (me + by) % size, 1, False), name, by)
    return total


def collect(values, name):
    size, me = lax.axis_size(name), lax.axis_index(name)
    result = jnp.zeros((size,) + values.shape, values.dtype)
    result = lax.dynamic_update_index_in_dim(result, values, me, 0)
    for by in range(1, size):
        result = lax.dynamic_update_index_in_dim(result, shifted(values, name, by), (me - by) % size, 0)
    return result


def collect_all(values):
    for name in ("lon", "lat", "lev"):
        values = collect(values, name)
    return values


def share_of(values):
    rows = values.reshape(values.shape[0], -1, LANES)
    for name in ("lev", "lat", "lon"):
        rows = share_sum(rows, name)
    return rows


def whole_of(share):
    for name in ("lon", "lat", "lev"):
        share = collect(share, name).reshape(-1, LANES)
    return share


def pick_kernel(nxt_ref, idx_ref, x_ref, e_ref, *moved_ref):
    members = e_ref.shape[3]
    batches, obs_total = idx_ref.shape[1:]
    lane = lax.broadcasted_iota(i32, (members, LANES), 1)
    if moved_ref:
        source = moved_ref[0]
        for slab in range(x_ref.shape[1]):
            source[slab] = x_ref[:, slab, :]
        source[x_ref.shape[1]] = jnp.zeros((members, LANES), f32)
    else:
        source = x_ref
    e_ref[...] = jnp.zeros_like(e_ref)

    for batch in range(batches):
        def step(i):
            block, column = i // LANES, i % LANES
            for corner in range(4):
                cell = idx_ref[corner, batch, i]
                held = cell >= 0
                safe = jnp.maximum(cell, 0)
                tile = source[safe // LANES]
                turned = pltpu.roll(tile, (column - safe % LANES + LANES) % LANES, 1)
                put = (lane == column) & held
                e_ref[batch, block, corner] = jnp.where(put, turned, e_ref[batch, block, corner])
            return nxt_ref[batch, i + 1]

        lax.while_loop(lambda i: i < obs_total, step, nxt_ref[batch, 0])


def lat_taper(rows, at, scale):
    gap = rows * scale - at
    return jnp.exp2(-(gap * gap))


def lon_taper(columns, at, scale, total):
    gap = jnp.abs(columns * scale - at)
    gap = jnp.minimum(gap, total * scale - gap)
    return jnp.exp2(-(gap * gap))


def scales(dims):
    return HALF_LOG2E**0.5 / dims[0], HALF_LOG2E**0.5 / (0.5 * dims[1])


def spread(row, scale):
    return jnp.broadcast_to(row * scale, (LANES, LANES)).T


def update(lhs1, lhs2, tiles, locality, bit=None):
    members = tiles[0].shape[0]
    pad = jnp.zeros((256 - 3 * members, LANES), bf16)
    columns = []
    for tile in tiles:
        high, low = split(tile)
        columns.append(jnp.concatenate([high, high, low, pad], axis=0))
    cov = jnp.dot(lhs1, jnp.concatenate(columns, axis=1), preferred_element_type=f32)
    columns = []
    for number in range(len(tiles)):
        gain = cov[:, number * LANES:(number + 1) * LANES] * locality(number)
        columns.append(jnp.concatenate(split(gain), axis=0))
    moved = jnp.dot(lhs2, jnp.concatenate(columns, axis=1), preferred_element_type=f32)
    results = []
    for number, tile in enumerate(tiles):
        lanes = slice(number * LANES, (number + 1) * LANES)
        change = moved[:members, lanes] + moved[members:, lanes]
        results.append(tile + (change if bit is None else change * bit(number)))
    return results


def stencil_kernel(dims, carried, where_ref, obs_ref, word_ref, e_in, *refs):
    if carried:
        carry_in, prior_ref, post_ref, lhs1_ref, lhs2_ref, carry_out = refs[:6]
    else:
        prior_ref, post_ref, lhs1_ref, lhs2_ref = refs[:4]
    e_ref, pos_ref = refs[-2:]
    lat_scale, lon_scale = scales(dims)
    lon_total = dims[2]
    blocks, members = e_in.shape[0], e_in.shape[2]
    keep, first = where_ref[2], where_ref[3]
    e_ref[0:blocks] = e_in[...]
    e_ref[blocks:] = jnp.zeros((2, 4, members, LANES), f32)
    if carried:
        for number in range(carried):
            e_ref[blocks + 1, first + number] = carry_in[number]
    pad_rows = 256 - 3 * members

    def observe(block):
        row = obs_ref[block]
        p, q = row[2:3], row[3:4]
        result = (1.0 - p) * (1.0 - q) * e_ref[block, 0]
        result = result + p * (1.0 - q) * e_ref[block, 1]
        result = result + (1.0 - p) * q * e_ref[block, 2]
        result = result + p * q * e_ref[block, 3]
        center = jnp.sum(result, axis=0, keepdims=True) / members
        anomaly = result - center
        variance = jnp.sum(anomaly * anomaly, axis=0, keepdims=True) / (members - 1) + epsilon
        return row, result, center, anomaly, variance

    def group_of(block, number):
        later = block + 1 + number
        kept = (keep <= block).astype(i32)
        end = jnp.where((later == blocks) & (kept == 1), keep, blocks)
        if carried:
            end = jnp.where(later == blocks + kept, blocks + 1, end)
        return jnp.where(later < blocks, later, end)

    def assimilate(block, carry):
        row, result, center, anomaly, variance = observe(block)
        y, r = row[4:5], row[5:6]
        denominator = variance + r
        post_mean = (center * r + y * variance) / denominator
        increment = post_mean + jnp.sqrt(r / denominator) * anomaly - result
        prior_ref[block] = jnp.concatenate([center, jnp.sqrt(variance)], axis=0)
        scaled = increment / (variance * (members - 1))
        r_high, r_low = split(scaled)
        lhs2_ref[block] = jnp.concatenate(
            [
                jnp.concatenate([r_high, r_high], axis=1),
                jnp.concatenate([r_low, jnp.zeros_like(r_low)], axis=1),
            ],
            axis=0,
        )
        d_high = anomaly.astype(bf16).astype(f32)
        d_low = anomaly - d_high
        packed = jnp.concatenate([d_high, d_low, d_high, jnp.zeros((pad_rows, LANES), f32)], axis=0)
        lhs1_ref[block] = packed.T.astype(bf16)
        pos_ref[0] = spread(row[0:1] + row[2:3], lat_scale)
        pos_ref[1] = spread(row[1:2] + row[3:4], lon_scale)

        def stencil(step, c):
            others = [group_of(block, step * GROUP + number) for number in range(GROUP)]
            la, lo = pos_ref[0], pos_ref[1]
            lats, lons, bits = [], [], []
            for other in others:
                orow = obs_ref[other]
                lats.append([lat_taper(orow[0:1], la, lat_scale), lat_taper(orow[0:1] + 1.0, la, lat_scale)])
                lons.append([lon_taper(orow[at:at + 1], lo, lon_scale, lon_total) for at in (1, 6)])
                bits.append(((word_ref[other] >> block) & 1).astype(f32))

            def locality(number):
                which, corner = number // 4, number % 4
                return lats[which][corner % 2] * lons[which][corner // 2]

            def bit(number):
                return bits[number // 4][number % 4:number % 4 + 1]

            tiles = [e_ref[other, corner] for other in others for corner in range(4)]
            for number, tile in enumerate(update(lhs1_ref[block], lhs2_ref[block], tiles, locality, bit)):
                e_ref[others[number // 4], number % 4] = tile
            return c

        pending = blocks - 1 - block + (keep <= block).astype(i32) + (1 if carried else 0)
        lax.fori_loop(0, pl.cdiv(pending, GROUP), stencil, 0)
        return carry

    lax.fori_loop(0, blocks, assimilate, 0)
    row, result, center, anomaly, variance = observe(keep)
    post_ref[...] = jnp.concatenate([center, jnp.sqrt(variance)], axis=0)
    if carried:
        for number in range(carried):
            carry_out[number] = e_ref[blocks + 1, first + number]


def own_kernel(dims, span, last, where_ref, count_ref, list_ref, obs_ref, lhs1_ref, lhs2_ref, x_ref, out_ref, loc_ref, *scratch):
    lat_scale, lon_scale = scales(dims)
    lat_dev, lon_dev, lon_total = dims
    lat_start, lon_start = where_ref[0], where_ref[1]
    state = scratch[0] if last else out_ref
    state[...] = x_ref[...]
    columns = (lon_start + lax.broadcasted_iota(i32, (LANES, LANES), 1)).astype(f32)

    def assimilate(block, carry):
        row = obs_ref[block]
        lat_at = spread(row[0:1] + row[2:3], lat_scale)
        own_lon = lon_taper(columns, spread(row[1:2] + row[3:4], lon_scale), lon_scale, lon_total)
        for a in range(lat_dev):
            loc_ref[a] = lat_taper((lat_start + a).astype(f32), lat_at, lat_scale) * own_lon

        def own(step, c):
            which = [list_ref[block, step * CHUNK + number] for number in range(CHUNK)]
            new = update(lhs1_ref[block], lhs2_ref[block], [state[w] for w in which],
                         lambda number: loc_ref[which[number] % lat_dev])
            for number in range(CHUNK):
                state[which[number]] = new[number]
            return c

        lax.fori_loop(0, pl.cdiv(count_ref[block], CHUNK), own, 0)
        return carry

    lax.fori_loop(span[0], span[1], assimilate, 0)
    if last:
        for slab in range(out_ref.shape[1]):
            out_ref[:, slab, :] = state[slab]


def word_kernel(slot_ref, table_ref, out_ref):
    for batch in range(slot_ref.shape[0]):
        slot = slot_ref[batch]
        place = slot % LANES
        row = slot // LANES
        result = jnp.zeros_like(slot)
        for number in range(table_ref.shape[1]):
            line = jnp.broadcast_to(table_ref[batch, number:number + 1], slot.shape)
            found = jnp.take_along_axis(line, place, axis=1)
            result = jnp.where(row == number, found, result)
        out_ref[batch] = result


def body(ensemble, obs_values, obs_error_var, obs_lat, obs_lon, obs_level, obs_frac, loc_mask):
    members, var_count, level_dev, lat_dev, lon_dev = ensemble.shape
    batches, blocks = loc_mask.shape[:2]
    obs_total = obs_values.shape[1]
    lat_parts, lon_parts, lev_parts = (lax.axis_size(name) for name in AXES)
    lat_at, lon_at, lev_at = (lax.axis_index(name) for name in AXES)
    lon_total, level_total, lat_total = lon_dev * lon_parts, level_dev * lev_parts, lat_dev * lat_parts
    lat_start, lon_start, level_start = lat_at * lat_dev, lon_at * lon_dev, lev_at * level_dev
    slabs = var_count * level_dev * lat_dev
    keep = (lat_at * lon_parts + lon_at) % blocks

    variable, level = obs_level // level_total, obs_level % level_total
    level_local = level - level_start
    cells, slots = [], []
    for row_step, col_step in ((0, 0), (1, 0), (0, 1), (1, 1)):
        row = obs_lat + row_step
        col = (obs_lon + col_step) % lon_total
        row_local, col_local = row - lat_start, col - lon_start
        held = (
            (level_local >= 0) & (level_local < level_dev) & (row_local >= 0) & (row_local < lat_dev)
            & (col_local >= 0) & (col_local < lon_dev)
        )
        cell = ((variable * level_dev + level_local) * lat_dev + row_local) * lon_dev + col_local
        cells.append(jnp.where(held, cell, -1))
        slots.append((obs_level * lat_total + row) * lon_parts + col // lon_dev)
    cells = jnp.stack(cells)
    slots = jnp.stack([slot.reshape(batches, blocks, LANES) for slot in slots], axis=2)
    spots = jnp.where(jnp.max(cells, axis=0) >= 0, jnp.arange(obs_total, dtype=i32), obs_total)
    grid = spots.reshape(batches, blocks, LANES)
    lane = jnp.arange(LANES)
    inside = jnp.min(jnp.where(lane[:, None] <= lane, grid[:, :, None, :], obs_total), axis=3)
    number = jnp.arange(blocks)
    beyond = jnp.min(jnp.where(number[:, None] < number, jnp.min(grid, axis=2)[:, None, :], obs_total), axis=2)
    nxt = jnp.minimum(inside, beyond[:, :, None]).reshape(batches, obs_total)
    nxt = jnp.concatenate([nxt, jnp.full((batches, 1), obs_total, i32)], axis=1)

    masks = collect_all(loc_mask.reshape(batches * blocks, slabs))
    masks = masks.reshape(lev_parts, lat_parts, lon_parts, batches, blocks, slabs)
    bits = jnp.sum(masks << jnp.arange(blocks, dtype=i32)[:, None], axis=4)
    bits = lax.optimization_barrier(bits).reshape(lev_parts, lat_parts, lon_parts, batches, var_count, level_dev, lat_dev)
    bits = bits.transpose(3, 4, 0, 5, 1, 6, 2).reshape(batches, -1)
    bits = jnp.pad(bits, ((0, 0), (0, -bits.shape[1] % LANES))).reshape(batches, -1, LANES)

    own = loc_mask.reshape(batches, blocks, slabs)
    count = jnp.sum(own, axis=2)
    rank = jnp.cumsum(own, axis=2) - 1
    padded = slabs + CHUNK
    hit = (rank[..., None] == jnp.arange(padded)) & (own[..., None] > 0)
    number = jnp.arange(slabs, dtype=i32)[:, None]
    active = slabs + jnp.sum(jnp.where(hit, number - slabs, 0), axis=2)

    def rows_of(values):
        return values.astype(f32).reshape(batches, blocks, LANES)

    obs_rows = jnp.stack(
        [rows_of(v) for v in (obs_lat, obs_lon, obs_frac[:, 0], obs_frac[:, 1], obs_values, obs_error_var,
                              (obs_lon + 1) % lon_total, obs_lat)],
        axis=2,
    )
    devices, tiles = lat_parts * lon_parts * lev_parts, 4 * blocks
    carry = tiles // devices if batches == 2 and tiles % devices == 0 and 4 % (tiles // devices) == 0 else 0
    first = ((lev_at * lat_parts + lat_at) * lon_parts + lon_at) * carry
    where = jnp.stack([lat_start, lon_start, keep, first % 4]).astype(i32)

    def extended(values):
        ahead = lax.dynamic_index_in_dim(values[-1], first // 4, 0, True)
        more = jnp.concatenate([jnp.zeros_like(ahead), ahead], axis=0)
        return jnp.concatenate([values, jnp.broadcast_to(more, (batches,) + more.shape)], axis=1)

    obs_rows, slots = extended(obs_rows), extended(slots)
    smem = pl.BlockSpec(memory_space=pltpu.SMEM)
    vmem = pl.BlockSpec(memory_space=pltpu.VMEM)
    params = pltpu.CompilerParams(vmem_limit_bytes=56 * 1024 * 1024)
    words = pl.pallas_call(
        word_kernel,
        out_shape=jax.ShapeDtypeStruct((batches, (blocks + 2) * 4, LANES), i32),
        in_specs=[vmem, vmem],
        out_specs=vmem,
    )(slots.reshape(batches, -1, LANES), bits).reshape(batches, blocks + 2, 4, LANES)
    state_shape = jax.ShapeDtypeStruct((slabs + 1, members, LANES), f32)
    natural_shape = jax.ShapeDtypeStruct((members, slabs, LANES), f32)

    def pick(which, x, natural):
        stencil_shape = jax.ShapeDtypeStruct((which.stop - which.start, blocks, 4, members, LANES), f32)
        return pl.pallas_call(
            pick_kernel,
            out_shape=(stencil_shape, state_shape) if natural else (stencil_shape,),
            in_specs=[smem, smem, vmem],
            out_specs=(vmem, vmem) if natural else (vmem,),
            compiler_params=params,
        )(nxt[which], cells[:, which], x)

    dims = (lat_dev, lon_dev, lon_total)

    def assimilate(batch, stencils, extra):
        shapes = (
            jax.ShapeDtypeStruct((blocks, 2, LANES), f32),
            jax.ShapeDtypeStruct((2, LANES), f32),
            jax.ShapeDtypeStruct((blocks, LANES, 256), bf16),
            jax.ShapeDtypeStruct((blocks, 2 * members, 256), bf16),
        )
        if extra:
            shapes += (jax.ShapeDtypeStruct((carry, members, LANES), f32),)
        return pl.pallas_call(
            functools.partial(stencil_kernel, dims, carry if extra else 0),
            out_shape=shapes,
            in_specs=[smem] + [vmem] * (3 + len(extra)),
            out_specs=(vmem,) * len(shapes),
            scratch_shapes=[
                pltpu.VMEM((blocks + 2, 4, members, LANES), f32),
                pltpu.VMEM((2, LANES, LANES), f32),
            ],
            compiler_params=params,
        )(where, obs_rows[batch], words[batch], stencils.reshape(blocks, 4, members, LANES), *extra)

    def advance(batch, x, factors, span):
        last = batch == batches - 1 and span[1] == blocks
        return pl.pallas_call(
            functools.partial(own_kernel, dims, span, last),
            out_shape=natural_shape if last else state_shape,
            in_specs=[smem] * 3 + [vmem] * 4,
            out_specs=vmem,
            scratch_shapes=[pltpu.VMEM((lat_dev, LANES, LANES), f32)]
            + ([pltpu.VMEM(state_shape.shape, f32)] if last else []),
            compiler_params=params,
        )(where, count[batch], active[batch], obs_rows[batch], *factors, x)

    natural = ensemble.reshape(members, slabs, LANES)
    picked, x = pick(slice(0, batches if carry else 1), natural, True)
    shares = share_of(picked)
    prior_parts, post_parts, stencils = [], [], whole_of(shares[0])
    for batch in range(batches):
        extra = (shares[1].reshape(carry, members, LANES),) if carry and batch == 0 else ()
        prior, post, *factors = assimilate(batch, stencils, extra)
        prior_parts.append(prior.transpose(1, 0, 2).reshape(2, obs_total))
        post_parts.append(post)
        if batch == batches - 1:
            rows, names, cuts = jnp.concatenate(post_parts, axis=0), ("lon", "lat"), (0, blocks // 2, blocks)
        elif carry:
            rows, names, cuts = factors.pop().reshape(-1, LANES), ("lon", "lat", "lev"), (0, blocks // 4, blocks * 13 // 16, blocks)
        else:
            x = advance(batch, x, factors, (0, blocks))
            stencils = whole_of(share_of(pick(slice(batch + 1, batch + 2), x, False)[0])[0])
            continue
        for name, start, stop in zip(names, cuts, cuts[1:]):
            rows = collect(rows, name).reshape(-1, LANES)
            x = advance(batch, x, factors, (start, stop))
            rows, x = lax.optimization_barrier((rows, x))
        stencils = rows
    posts = stencils.reshape(-1, 2 * batches, LANES)[:blocks]
    posts = posts.transpose(1, 0, 2).reshape(batches, 2, obs_total)
    return x.reshape(ensemble.shape), jnp.stack(prior_parts), posts


def solution(mesh):
    state = P(None, None, "lev", "lat", "lon")
    return jax.shard_map(
        body,
        mesh=mesh,
        in_specs=(state, P(), P(), P(), P(), P(), P(), P(None, None, None, "lev", "lat", "lon")),
        out_specs=(state, P(), P()),
        check_vma=False,
    )
```

```python
import functools

import jax
import jax.numpy as jnp
from jax import lax
from jax.experimental import pallas as pl
from jax.experimental.pallas import tpu as pltpu
from jax.sharding import PartitionSpec as P

epsilon = 1e-06
AXES = ("lat", "lon", "lev")
LANES = 128
CHUNK = 20
HALF_LOG2E = 0.7213475204444817
GROUP = 3
PICKS = 2
f32, bf16, i32 = jnp.float32, jnp.bfloat16, jnp.int32


def split(values):
    high = values.astype(bf16)
    return high, (values - high.astype(f32)).astype(bf16)


def shifted(values, name, by):
    size = lax.axis_size(name)
    return lax.ppermute(values, name, [(i, (i + by) % size) for i in range(size)])


def share_sum(values, name):
    size, me = lax.axis_size(name), lax.axis_index(name)
    parts = values.reshape(values.shape[0], size, -1, LANES)
    total = lax.dynamic_index_in_dim(parts, me, 1, False)
    for by in range(1, size):
        total = total + shifted(lax.dynamic_index_in_dim(parts, (me + by) % size, 1, False), name, by)
    return total


def collect(values, name):
    size, me = lax.axis_size(name), lax.axis_index(name)
    result = jnp.zeros((size,) + values.shape, values.dtype)
    result = lax.dynamic_update_index_in_dim(result, values, me, 0)
    for by in range(1, size):
        result = lax.dynamic_update_index_in_dim(result, shifted(values, name, by), (me - by) % size, 0)
    return result


def collect_all(values):
    for name in ("lon", "lat", "lev"):
        values = collect(values, name)
    return values


def share_of(values):
    rows = values.reshape(values.shape[0], -1, LANES)
    for name in ("lev", "lat", "lon"):
        rows = share_sum(rows, name)
    return rows


def whole_of(share):
    for name in ("lon", "lat", "lev"):
        share = collect(share, name).reshape(-1, LANES)
    return share


def pick_kernel(nxt_ref, idx_ref, x_ref, e_ref, *moved_ref):
    members = e_ref.shape[3]
    batches, obs_total = idx_ref.shape[1:]
    lane = lax.broadcasted_iota(i32, (members, LANES), 1)
    if moved_ref:
        source = moved_ref[0]
        for slab in range(x_ref.shape[1]):
            source[slab] = x_ref[:, slab, :]
        source[x_ref.shape[1]] = jnp.zeros((members, LANES), f32)
    else:
        source = x_ref
    e_ref[...] = jnp.zeros_like(e_ref)

    for batch in range(batches):
        def step(i):
            turned, put, spots = [], [], []
            for _ in range(PICKS):
                now = jnp.minimum(i, obs_total - 1)
                block, column = now // LANES, now % LANES
                for corner in range(4):
                    cell = idx_ref[corner, batch, now]
                    safe = jnp.maximum(cell, 0)
                    turned.append(pltpu.roll(source[safe // LANES], (column - safe % LANES + LANES) % LANES, 1))
                    put.append((lane == column) & (cell >= 0))
                    spots.append((block, corner))
                i = nxt_ref[batch, jnp.minimum(i + 1, obs_total)]
            for (block, corner), value, mask in zip(spots, turned, put):
                pltpu.store(e_ref.at[batch, block, corner], value, mask=mask)
            return i

        lax.while_loop(lambda i: i < obs_total, step, nxt_ref[batch, 0])


def lat_taper(rows, at, scale):
    gap = rows * scale - at
    return jnp.exp2(-(gap * gap))


def lon_taper(columns, at, scale, total):
    gap = jnp.abs(columns * scale - at)
    gap = jnp.minimum(gap, total * scale - gap)
    return jnp.exp2(-(gap * gap))


def scales(dims):
    return HALF_LOG2E**0.5 / dims[0], HALF_LOG2E**0.5 / (0.5 * dims[1])


def spread(row, scale):
    return jnp.broadcast_to(row * scale, (LANES, LANES)).T


def update(lhs1, lhs2, tiles, locality, bit=None):
    members = tiles[0].shape[0]
    pad = jnp.zeros((256 - 3 * members, LANES), bf16)
    columns = []
    for tile in tiles:
        high, low = split(tile)
        columns.append(jnp.concatenate([high, high, low, pad], axis=0))
    cov = jnp.dot(lhs1, jnp.concatenate(columns, axis=1), preferred_element_type=f32)
    columns = []
    for number in range(len(tiles)):
        gain = cov[:, number * LANES:(number + 1) * LANES] * locality(number)
        columns.append(jnp.concatenate(split(gain), axis=0))
    moved = jnp.dot(lhs2, jnp.concatenate(columns, axis=1), preferred_element_type=f32)
    results = []
    for number, tile in enumerate(tiles):
        lanes = slice(number * LANES, (number + 1) * LANES)
        change = moved[:members, lanes] + moved[members:, lanes]
        results.append(tile + (change if bit is None else change * bit(number)))
    return results


def stencil_kernel(dims, where_ref, obs_ref, word_ref, e_in, prior_ref, post_ref, lhs1_ref, lhs2_ref, e_ref, pos_ref):
    lat_scale, lon_scale = scales(dims)
    lon_total = dims[2]
    blocks, members = e_in.shape[0], e_in.shape[2]
    keep = where_ref[2]
    e_ref[0:blocks] = e_in[...]
    e_ref[blocks] = jnp.zeros((4, members, LANES), f32)
    pad_rows = 256 - 3 * members

    def observe(block):
        row = obs_ref[block]
        p, q = row[2:3], row[3:4]
        result = (1.0 - p) * (1.0 - q) * e_ref[block, 0]
        result = result + p * (1.0 - q) * e_ref[block, 1]
        result = result + (1.0 - p) * q * e_ref[block, 2]
        result = result + p * q * e_ref[block, 3]
        center = jnp.sum(result, axis=0, keepdims=True) / members
        anomaly = result - center
        variance = jnp.sum(anomaly * anomaly, axis=0, keepdims=True) / (members - 1) + epsilon
        return row, result, center, anomaly, variance

    def group_of(block, number):
        later = block + 1 + number
        end = jnp.where((later == blocks) & (keep <= block), keep, blocks)
        return jnp.where(later < blocks, later, end)

    def assimilate(block, carry):
        row, result, center, anomaly, variance = observe(block)
        y, r = row[4:5], row[5:6]
        denominator = variance + r
        post_mean = (center * r + y * variance) / denominator
        increment = post_mean + jnp.sqrt(r / denominator) * anomaly - result
        prior_ref[block] = jnp.concatenate([center, jnp.sqrt(variance)], axis=0)
        scaled = increment / (variance * (members - 1))
        r_high, r_low = split(scaled)
        lhs2_ref[block] = jnp.concatenate(
            [
                jnp.concatenate([r_high, r_high], axis=1),
                jnp.concatenate([r_low, jnp.zeros_like(r_low)], axis=1),
            ],
            axis=0,
        )
        d_high = anomaly.astype(bf16).astype(f32)
        d_low = anomaly - d_high
        packed = jnp.concatenate([d_high, d_low, d_high, jnp.zeros((pad_rows, LANES), f32)], axis=0)
        lhs1_ref[block] = packed.T.astype(bf16)
        pos_ref[0] = spread(row[0:1] + row[2:3], lat_scale)
        pos_ref[1] = spread(row[1:2] + row[3:4], lon_scale)

        def stencil(step, c):
            others = [group_of(block, step * GROUP + number) for number in range(GROUP)]
            la, lo = pos_ref[0], pos_ref[1]
            lats, lons, bits = [], [], []
            for other in others:
                orow = obs_ref[other]
                lats.append([lat_taper(orow[0:1], la, lat_scale), lat_taper(orow[0:1] + 1.0, la, lat_scale)])
                lons.append([lon_taper(orow[at:at + 1], lo, lon_scale, lon_total) for at in (1, 6)])
                bits.append(((word_ref[other] >> block) & 1).astype(f32))

            def locality(number):
                which, corner = number // 4, number % 4
                return lats[which][corner % 2] * lons[which][corner // 2]

            def bit(number):
                return bits[number // 4][number % 4:number % 4 + 1]

            tiles = [e_ref[other, corner] for other in others for corner in range(4)]
            for number, tile in enumerate(update(lhs1_ref[block], lhs2_ref[block], tiles, locality, bit)):
                e_ref[others[number // 4], number % 4] = tile
            return c

        pending = blocks - 1 - block + (keep <= block).astype(i32)
        lax.fori_loop(0, pl.cdiv(pending, GROUP), stencil, 0)
        return carry

    lax.fori_loop(0, blocks, assimilate, 0)
    row, result, center, anomaly, variance = observe(keep)
    post_ref[...] = jnp.concatenate([center, jnp.sqrt(variance)], axis=0)


def carry_kernel(dims, where_ref, obs_ref, word_ref, lhs1_ref, lhs2_ref, in_ref, out_ref):
    lat_scale, lon_scale = scales(dims)
    blocks, first = lhs1_ref.shape[0], where_ref[3]
    out_ref[...] = in_ref[...]
    orow, words = obs_ref[blocks + 1], word_ref[blocks + 1]
    rows, columns, masks = [], [], []
    for number in range(in_ref.shape[0]):
        corner = first + number
        rows.append(orow[0:1] + (corner % 2).astype(f32))
        columns.append(jnp.where(corner // 2 == 0, orow[1:2], orow[6:7]))
        masks.append(sum(jnp.where(corner == c, words[c:c + 1], 0) for c in range(4)))

    def assimilate(block):
        row = obs_ref[block]
        lat_at = spread(row[0:1] + row[2:3], lat_scale)
        lon_at = spread(row[1:2] + row[3:4], lon_scale)
        near = [lat_taper(r, lat_at, lat_scale) * lon_taper(c, lon_at, lon_scale, dims[2]) for r, c in zip(rows, columns)]
        bits = [((mask >> block) & 1).astype(f32) for mask in masks]
        tiles = [out_ref[number] for number in range(len(rows))]
        new = update(lhs1_ref[block], lhs2_ref[block], tiles, lambda n: near[n], lambda n: bits[n])
        for number, tile in enumerate(new):
            out_ref[number] = tile

    def several(step, c):
        for number in range(4):
            assimilate(step * 4 + number)
        return c

    lax.fori_loop(0, blocks // 4, several, 0)


def own_kernel(dims, span, last, where_ref, count_ref, list_ref, obs_ref, lhs1_ref, lhs2_ref, x_ref, out_ref, loc_ref, *scratch):
    lat_scale, lon_scale = scales(dims)
    lat_dev, lon_dev, lon_total = dims
    lat_start, lon_start = where_ref[0], where_ref[1]
    state = scratch[0] if last else out_ref
    state[...] = x_ref[...]
    columns = (lon_start + lax.broadcasted_iota(i32, (LANES, LANES), 1)).astype(f32)

    def assimilate(block, carry):
        row = obs_ref[block]
        lat_at = spread(row[0:1] + row[2:3], lat_scale)
        own_lon = lon_taper(columns, spread(row[1:2] + row[3:4], lon_scale), lon_scale, lon_total)
        for a in range(lat_dev):
            loc_ref[a] = lat_taper((lat_start + a).astype(f32), lat_at, lat_scale) * own_lon

        def own(step, c):
            which = [list_ref[block, step * CHUNK + number] for number in range(CHUNK)]
            new = update(lhs1_ref[block], lhs2_ref[block], [state[w] for w in which],
                         lambda number: loc_ref[which[number] % lat_dev])
            for number in range(CHUNK):
                state[which[number]] = new[number]
            return c

        lax.fori_loop(0, pl.cdiv(count_ref[block], CHUNK), own, 0)
        return carry

    lax.fori_loop(span[0], span[1], assimilate, 0)
    if last:
        for slab in range(out_ref.shape[1]):
            out_ref[:, slab, :] = state[slab]


def word_kernel(slot_ref, table_ref, out_ref):
    for batch in range(slot_ref.shape[0]):
        slot = slot_ref[batch]
        place = slot % LANES
        row = slot // LANES
        result = jnp.zeros_like(slot)
        for number in range(table_ref.shape[1]):
            line = jnp.broadcast_to(table_ref[batch, number:number + 1], slot.shape)
            found = jnp.take_along_axis(line, place, axis=1)
            result = jnp.where(row == number, found, result)
        out_ref[batch] = result


def body(ensemble, obs_values, obs_error_var, obs_lat, obs_lon, obs_level, obs_frac, loc_mask):
    members, var_count, level_dev, lat_dev, lon_dev = ensemble.shape
    batches, blocks = loc_mask.shape[:2]
    obs_total = obs_values.shape[1]
    lat_parts, lon_parts, lev_parts = (lax.axis_size(name) for name in AXES)
    lat_at, lon_at, lev_at = (lax.axis_index(name) for name in AXES)
    lon_total, level_total, lat_total = lon_dev * lon_parts, level_dev * lev_parts, lat_dev * lat_parts
    lat_start, lon_start, level_start = lat_at * lat_dev, lon_at * lon_dev, lev_at * level_dev
    slabs = var_count * level_dev * lat_dev
    keep = (lat_at * lon_parts + lon_at) % blocks

    variable, level = obs_level // level_total, obs_level % level_total
    level_local = level - level_start
    cells, slots = [], []
    for row_step, col_step in ((0, 0), (1, 0), (0, 1), (1, 1)):
        row = obs_lat + row_step
        col = (obs_lon + col_step) % lon_total
        row_local, col_local = row - lat_start, col - lon_start
        held = (
            (level_local >= 0) & (level_local < level_dev) & (row_local >= 0) & (row_local < lat_dev)
            & (col_local >= 0) & (col_local < lon_dev)
        )
        cell = ((variable * level_dev + level_local) * lat_dev + row_local) * lon_dev + col_local
        cells.append(jnp.where(held, cell, -1))
        slots.append((obs_level * lat_total + row) * lon_parts + col // lon_dev)
    cells = jnp.stack(cells)
    slots = jnp.stack([slot.reshape(batches, blocks, LANES) for slot in slots], axis=2)
    spots = jnp.where(jnp.max(cells, axis=0) >= 0, jnp.arange(obs_total, dtype=i32), obs_total)
    grid = spots.reshape(batches, blocks, LANES)
    lane = jnp.arange(LANES)
    inside = jnp.min(jnp.where(lane[:, None] <= lane, grid[:, :, None, :], obs_total), axis=3)
    number = jnp.arange(blocks)
    beyond = jnp.min(jnp.where(number[:, None] < number, jnp.min(grid, axis=2)[:, None, :], obs_total), axis=2)
    nxt = jnp.minimum(inside, beyond[:, :, None]).reshape(batches, obs_total)
    nxt = jnp.concatenate([nxt, jnp.full((batches, 1), obs_total, i32)], axis=1)

    own = loc_mask.reshape(batches, blocks, slabs)
    count = jnp.sum(own, axis=2)
    rank = jnp.cumsum(own, axis=2) - 1
    padded = slabs + CHUNK
    hit = (rank[..., None] == jnp.arange(padded)) & (own[..., None] > 0)
    number = jnp.arange(slabs, dtype=i32)[:, None]
    active = slabs + jnp.sum(jnp.where(hit, number - slabs, 0), axis=2)

    def rows_of(values):
        return values.astype(f32).reshape(batches, blocks, LANES)

    obs_rows = jnp.stack(
        [rows_of(v) for v in (obs_lat, obs_lon, obs_frac[:, 0], obs_frac[:, 1], obs_values, obs_error_var,
                              (obs_lon + 1) % lon_total, obs_lat)],
        axis=2,
    )
    devices, tiles = lat_parts * lon_parts * lev_parts, 4 * blocks
    carry = tiles // devices if batches == 2 and tiles % devices == 0 and 4 % (tiles // devices) == 0 else 0
    first = ((lev_at * lat_parts + lat_at) * lon_parts + lon_at) * carry
    where = jnp.stack([lat_start, lon_start, keep, first % 4]).astype(i32)

    def extended(values):
        ahead = lax.dynamic_index_in_dim(values[-1], first // 4, 0, True)
        more = jnp.concatenate([jnp.zeros_like(ahead), ahead], axis=0)
        return jnp.concatenate([values, jnp.broadcast_to(more, (batches,) + more.shape)], axis=1)

    obs_rows, slots = extended(obs_rows), extended(slots)
    smem = pl.BlockSpec(memory_space=pltpu.SMEM)
    vmem = pl.BlockSpec(memory_space=pltpu.VMEM)
    params = pltpu.CompilerParams(vmem_limit_bytes=56 * 1024 * 1024)
    state_shape = jax.ShapeDtypeStruct((slabs + 1, members, LANES), f32)
    natural_shape = jax.ShapeDtypeStruct((members, slabs, LANES), f32)

    def pick(which, x, natural):
        stencil_shape = jax.ShapeDtypeStruct((which.stop - which.start, blocks, 4, members, LANES), f32)
        return pl.pallas_call(
            pick_kernel,
            out_shape=(stencil_shape, state_shape) if natural else (stencil_shape,),
            in_specs=[smem, smem, vmem],
            out_specs=(vmem, vmem) if natural else (vmem,),
            compiler_params=params,
        )(nxt[which], cells[:, which], x)

    dims = (lat_dev, lon_dev, lon_total)

    def assimilate(batch, stencils):
        shapes = (
            jax.ShapeDtypeStruct((blocks, 2, LANES), f32),
            jax.ShapeDtypeStruct((2, LANES), f32),
            jax.ShapeDtypeStruct((blocks, LANES, 256), bf16),
            jax.ShapeDtypeStruct((blocks, 2 * members, 256), bf16),
        )
        return pl.pallas_call(
            functools.partial(stencil_kernel, dims),
            out_shape=shapes,
            in_specs=[smem] + [vmem] * 3,
            out_specs=(vmem,) * len(shapes),
            scratch_shapes=[
                pltpu.VMEM((blocks + 1, 4, members, LANES), f32),
                pltpu.VMEM((2, LANES, LANES), f32),
            ],
            compiler_params=params,
        )(where, obs_rows[batch], words[batch], stencils.reshape(blocks, 4, members, LANES))

    def bring(batch, share, factors):
        return pl.pallas_call(
            functools.partial(carry_kernel, dims),
            out_shape=jax.ShapeDtypeStruct((carry, members, LANES), f32),
            in_specs=[smem] + [vmem] * 5,
            out_specs=vmem,
            compiler_params=params,
        )(where, obs_rows[batch], words[batch], *factors, share.reshape(carry, members, LANES)).reshape(-1, LANES)

    def advance(batch, x, factors, span):
        last = batch == batches - 1 and span[1] == blocks
        return pl.pallas_call(
            functools.partial(own_kernel, dims, span, last),
            out_shape=natural_shape if last else state_shape,
            in_specs=[smem] * 3 + [vmem] * 4,
            out_specs=vmem,
            scratch_shapes=[pltpu.VMEM((lat_dev, LANES, LANES), f32)]
            + ([pltpu.VMEM(state_shape.shape, f32)] if last else []),
            compiler_params=params,
        )(where, count[batch], active[batch], obs_rows[batch], *factors, x)

    natural = ensemble.reshape(members, slabs, LANES)
    together = lax.optimization_barrier
    picked, x = pick(slice(0, 1), natural, True)
    picked, loc_mask = together((picked, loc_mask))
    masks = collect_all(loc_mask.reshape(batches * blocks, slabs))
    masks = masks.reshape(lev_parts, lat_parts, lon_parts, batches, blocks, slabs)
    bits = jnp.sum(masks << jnp.arange(blocks, dtype=i32)[:, None], axis=4)
    bits = lax.optimization_barrier(bits).reshape(lev_parts, lat_parts, lon_parts, batches, var_count, level_dev, lat_dev)
    bits = bits.transpose(3, 4, 0, 5, 1, 6, 2).reshape(batches, -1)
    bits = jnp.pad(bits, ((0, 0), (0, -bits.shape[1] % LANES))).reshape(batches, -1, LANES)
    words = pl.pallas_call(
        word_kernel,
        out_shape=jax.ShapeDtypeStruct((batches, (blocks + 2) * 4, LANES), i32),
        in_specs=[vmem, vmem],
        out_specs=vmem,
    )(slots.reshape(batches, -1, LANES), bits).reshape(batches, blocks + 2, 4, LANES)
    share = share_sum(picked.reshape(1, -1, LANES), "lev")
    if carry:
        share, x = together((share, x))
        ahead = pick(slice(1, 2), x, False)[0].reshape(1, -1, LANES)
    share = share_sum(share, "lat")
    if carry:
        share, ahead, words = together((share, ahead, words))
        ahead = share_sum(ahead, "lev")
    share = share_sum(share, "lon")[0]
    stencils = collect(collect(share, "lon").reshape(-1, LANES), "lat").reshape(-1, LANES)
    if carry:
        stencils, ahead = together((stencils, ahead))
    stencils = collect(stencils, "lev")
    if carry:
        stencils, ahead = together((stencils, ahead))
    prior_parts, post_parts = [], []
    for batch in range(batches):
        prior, post, *factors = assimilate(batch, stencils)
        prior_parts.append(prior.transpose(1, 0, 2).reshape(2, obs_total))
        post_parts.append(post)
        if batch == batches - 1:
            rows, names, cuts = jnp.concatenate(post_parts, axis=0), ("lon", "lat"), (0, blocks // 2, blocks)
        elif carry:
            ahead = share_sum(ahead, "lat")
            ahead, factors = together((ahead, factors))
            ahead = share_sum(ahead, "lon")
            x = advance(batch, x, factors, (0, blocks // 4))
            ahead, x = together((ahead, x))
            rows = bring(batch, ahead, factors)
            names, cuts = ("lon", "lat", "lev"), (blocks // 4, blocks * 7 // 16, blocks * 7 // 8, blocks)
        else:
            x = advance(batch, x, factors, (0, blocks))
            stencils = whole_of(share_of(pick(slice(batch + 1, batch + 2), x, False)[0])[0])
            continue
        for name, start, stop in zip(names, cuts, cuts[1:]):
            rows = collect(rows, name).reshape(-1, LANES)
            x = advance(batch, x, factors, (start, stop))
            rows, x = together((rows, x))
        stencils = rows
    posts = stencils.reshape(-1, 2 * batches, LANES)[:blocks]
    posts = posts.transpose(1, 0, 2).reshape(batches, 2, obs_total)
    return x.reshape(ensemble.shape), jnp.stack(prior_parts), posts


def solution(mesh):
    state = P(None, None, "lev", "lat", "lon")
    return jax.shard_map(
        body,
        mesh=mesh,
        in_specs=(state, P(), P(), P(), P(), P(), P(), P(None, None, None, "lev", "lat", "lon")),
        out_specs=(state, P(), P()),
        check_vma=False,
    )
```

```python
import functools

import jax
import jax.numpy as jnp
from jax import lax
from jax.experimental import pallas as pl
from jax.experimental.pallas import tpu as pltpu
from jax.sharding import PartitionSpec as P

epsilon = 1e-06
AXES = ("lat", "lon", "lev")
LANES = 128
CHUNK = 20
HALF_LOG2E = 0.7213475204444817
GROUP = 3
PICKS = 2
f32, bf16, i32 = jnp.float32, jnp.bfloat16, jnp.int32


def split(values):
    high = values.astype(bf16)
    return high, (values - high.astype(f32)).astype(bf16)


def shifted(values, name, by):
    size = lax.axis_size(name)
    return lax.ppermute(values, name, [(i, (i + by) % size) for i in range(size)])


def share_sum(values, name):
    size, me = lax.axis_size(name), lax.axis_index(name)
    parts = values.reshape(values.shape[0], size, -1, LANES)
    total = lax.dynamic_index_in_dim(parts, me, 1, False)
    for by in range(1, size):
        total = total + shifted(lax.dynamic_index_in_dim(parts, (me + by) % size, 1, False), name, by)
    return total


def collect(values, name):
    size, me = lax.axis_size(name), lax.axis_index(name)
    result = jnp.zeros((size,) + values.shape, values.dtype)
    result = lax.dynamic_update_index_in_dim(result, values, me, 0)
    for by in range(1, size):
        result = lax.dynamic_update_index_in_dim(result, shifted(values, name, by), (me - by) % size, 0)
    return result


def share_of(values):
    rows = values.reshape(values.shape[0], -1, LANES)
    for name in ("lev", "lat", "lon"):
        rows = share_sum(rows, name)
    return rows


def whole_of(share):
    for name in ("lon", "lat", "lev"):
        share = collect(share, name).reshape(-1, LANES)
    return share


def pick_kernel(nxt_ref, idx_ref, x_ref, e_ref, *moved_ref):
    members = e_ref.shape[3]
    batches, obs_total = idx_ref.shape[1:]
    lane = lax.broadcasted_iota(i32, (members, LANES), 1)
    if moved_ref:
        source = moved_ref[0]
        for slab in range(x_ref.shape[1]):
            source[slab] = x_ref[:, slab, :]
        source[x_ref.shape[1]] = jnp.zeros((members, LANES), f32)
    else:
        source = x_ref
    e_ref[...] = jnp.zeros_like(e_ref)

    for batch in range(batches):
        def step(i):
            turned, put, spots = [], [], []
            for _ in range(PICKS):
                now = jnp.minimum(i, obs_total - 1)
                block, column = now // LANES, now % LANES
                for corner in range(4):
                    cell = idx_ref[corner, batch, now]
                    safe = jnp.maximum(cell, 0)
                    turned.append(pltpu.roll(source[safe // LANES], (column - safe % LANES + LANES) % LANES, 1))
                    put.append((lane == column) & (cell >= 0))
                    spots.append((block, corner))
                i = nxt_ref[batch, jnp.minimum(i + 1, obs_total)]
            for (block, corner), value, mask in zip(spots, turned, put):
                pltpu.store(e_ref.at[batch, block, corner], value, mask=mask)
            return i

        lax.while_loop(lambda i: i < obs_total, step, nxt_ref[batch, 0])


def lat_taper(rows, at, scale):
    gap = rows * scale - at
    return jnp.exp2(-(gap * gap))


def lon_taper(columns, at, scale, total):
    gap = jnp.abs(columns * scale - at)
    gap = jnp.minimum(gap, total * scale - gap)
    return jnp.exp2(-(gap * gap))


def scales(dims):
    return HALF_LOG2E**0.5 / dims[0], HALF_LOG2E**0.5 / (0.5 * dims[1])


def spread(row, scale):
    return jnp.broadcast_to(row * scale, (LANES, LANES)).T


def update(lhs1, lhs2, tiles, locality, bit=None):
    members = tiles[0].shape[0]
    pad = jnp.zeros((256 - 3 * members, LANES), bf16)
    columns = []
    for tile in tiles:
        high, low = split(tile)
        columns.append(jnp.concatenate([high, high, low, pad], axis=0))
    cov = jnp.dot(lhs1, jnp.concatenate(columns, axis=1), preferred_element_type=f32)
    columns = []
    for number in range(len(tiles)):
        gain = cov[:, number * LANES:(number + 1) * LANES] * locality(number)
        columns.append(jnp.concatenate(split(gain), axis=0))
    moved = jnp.dot(lhs2, jnp.concatenate(columns, axis=1), preferred_element_type=f32)
    results = []
    for number, tile in enumerate(tiles):
        lanes = slice(number * LANES, (number + 1) * LANES)
        change = moved[:members, lanes] + moved[members:, lanes]
        results.append(tile + (change if bit is None else change * bit(number)))
    return results


def stencil_kernel(dims, where_ref, obs_ref, word_ref, e_in, prior_ref, post_ref, lhs1_ref, lhs2_ref, e_ref, pos_ref):
    lat_scale, lon_scale = scales(dims)
    lon_total = dims[2]
    blocks, members = e_in.shape[0], e_in.shape[2]
    keep = where_ref[2]
    e_ref[0:blocks] = e_in[...]
    e_ref[blocks] = jnp.zeros((4, members, LANES), f32)
    pad_rows = 256 - 3 * members

    def observe(block):
        row = obs_ref[block]
        p, q = row[2:3], row[3:4]
        result = (1.0 - p) * (1.0 - q) * e_ref[block, 0]
        result = result + p * (1.0 - q) * e_ref[block, 1]
        result = result + (1.0 - p) * q * e_ref[block, 2]
        result = result + p * q * e_ref[block, 3]
        center = jnp.sum(result, axis=0, keepdims=True) / members
        anomaly = result - center
        variance = jnp.sum(anomaly * anomaly, axis=0, keepdims=True) / (members - 1) + epsilon
        return row, result, center, anomaly, variance

    def group_of(block, number):
        later = block + 1 + number
        end = jnp.where((later == blocks) & (keep <= block), keep, blocks)
        return jnp.where(later < blocks, later, end)

    def assimilate(block, carry):
        row, result, center, anomaly, variance = observe(block)
        y, r = row[4:5], row[5:6]
        denominator = variance + r
        post_mean = (center * r + y * variance) / denominator
        increment = post_mean + jnp.sqrt(r / denominator) * anomaly - result
        prior_ref[block] = jnp.concatenate([center, jnp.sqrt(variance)], axis=0)
        scaled = increment / (variance * (members - 1))
        r_high, r_low = split(scaled)
        lhs2_ref[block] = jnp.concatenate(
            [
                jnp.concatenate([r_high, r_high], axis=1),
                jnp.concatenate([r_low, jnp.zeros_like(r_low)], axis=1),
            ],
            axis=0,
        )
        d_high = anomaly.astype(bf16).astype(f32)
        d_low = anomaly - d_high
        packed = jnp.concatenate([d_high, d_low, d_high, jnp.zeros((pad_rows, LANES), f32)], axis=0)
        lhs1_ref[block] = packed.T.astype(bf16)
        pos_ref[0] = spread(row[0:1] + row[2:3], lat_scale)
        pos_ref[1] = spread(row[1:2] + row[3:4], lon_scale)

        def stencil(step, c):
            others = [group_of(block, step * GROUP + number) for number in range(GROUP)]
            la, lo = pos_ref[0], pos_ref[1]
            lats, lons, bits = [], [], []
            for other in others:
                orow = obs_ref[other]
                lats.append([lat_taper(orow[0:1], la, lat_scale), lat_taper(orow[0:1] + 1.0, la, lat_scale)])
                lons.append([lon_taper(orow[at:at + 1], lo, lon_scale, lon_total) for at in (1, 6)])
                bits.append(((word_ref[other] >> block) & 1).astype(f32))

            def locality(number):
                which, corner = number // 4, number % 4
                return lats[which][corner % 2] * lons[which][corner // 2]

            def bit(number):
                return bits[number // 4][number % 4:number % 4 + 1]

            tiles = [e_ref[other, corner] for other in others for corner in range(4)]
            for number, tile in enumerate(update(lhs1_ref[block], lhs2_ref[block], tiles, locality, bit)):
                e_ref[others[number // 4], number % 4] = tile
            return c

        pending = blocks - 1 - block + (keep <= block).astype(i32)
        lax.fori_loop(0, pl.cdiv(pending, GROUP), stencil, 0)
        return carry

    lax.fori_loop(0, blocks, assimilate, 0)
    row, result, center, anomaly, variance = observe(keep)
    post_ref[...] = jnp.concatenate([center, jnp.sqrt(variance)], axis=0)


def carry_kernel(dims, where_ref, obs_ref, word_ref, lhs1_ref, lhs2_ref, in_ref, out_ref):
    lat_scale, lon_scale = scales(dims)
    blocks, first = lhs1_ref.shape[0], where_ref[3]
    out_ref[...] = in_ref[...]
    orow, words = obs_ref[blocks + 1], word_ref[blocks + 1]
    rows, columns, masks = [], [], []
    for number in range(in_ref.shape[0]):
        corner = first + number
        rows.append(orow[0:1] + (corner % 2).astype(f32))
        columns.append(jnp.where(corner // 2 == 0, orow[1:2], orow[6:7]))
        masks.append(sum(jnp.where(corner == c, words[c:c + 1], 0) for c in range(4)))

    def assimilate(block):
        row = obs_ref[block]
        lat_at = spread(row[0:1] + row[2:3], lat_scale)
        lon_at = spread(row[1:2] + row[3:4], lon_scale)
        near = [lat_taper(r, lat_at, lat_scale) * lon_taper(c, lon_at, lon_scale, dims[2]) for r, c in zip(rows, columns)]
        bits = [((mask >> block) & 1).astype(f32) for mask in masks]
        tiles = [out_ref[number] for number in range(len(rows))]
        new = update(lhs1_ref[block], lhs2_ref[block], tiles, lambda n: near[n], lambda n: bits[n])
        for number, tile in enumerate(new):
            out_ref[number] = tile

    def several(step, c):
        for number in range(4):
            assimilate(step * 4 + number)
        return c

    lax.fori_loop(0, blocks // 4, several, 0)


def own_kernel(dims, span, last, where_ref, count_ref, list_ref, obs_ref, lhs1_ref, lhs2_ref, x_ref, out_ref, loc_ref, *scratch):
    lat_scale, lon_scale = scales(dims)
    lat_dev, lon_dev, lon_total = dims
    lat_start, lon_start = where_ref[0], where_ref[1]
    state = scratch[0] if last else out_ref
    state[...] = x_ref[...]
    columns = (lon_start + lax.broadcasted_iota(i32, (LANES, LANES), 1)).astype(f32)

    def assimilate(block, carry):
        row = obs_ref[block]
        lat_at = spread(row[0:1] + row[2:3], lat_scale)
        own_lon = lon_taper(columns, spread(row[1:2] + row[3:4], lon_scale), lon_scale, lon_total)
        for a in range(lat_dev):
            loc_ref[a] = lat_taper((lat_start + a).astype(f32), lat_at, lat_scale) * own_lon

        def own(step, c):
            which = [list_ref[block, step * CHUNK + number] for number in range(CHUNK)]
            new = update(lhs1_ref[block], lhs2_ref[block], [state[w] for w in which],
                         lambda number: loc_ref[which[number] % lat_dev])
            for number in range(CHUNK):
                state[which[number]] = new[number]
            return c

        lax.fori_loop(0, pl.cdiv(count_ref[block], CHUNK), own, 0)
        return carry

    lax.fori_loop(span[0], span[1], assimilate, 0)
    if last:
        for slab in range(out_ref.shape[1]):
            out_ref[:, slab, :] = state[slab]


def word_kernel(slot_ref, table_ref, out_ref):
    for batch in range(slot_ref.shape[0]):
        slot = slot_ref[batch]
        place = slot % LANES
        row = slot // LANES
        result = jnp.zeros_like(slot)
        for number in range(table_ref.shape[1]):
            line = jnp.broadcast_to(table_ref[batch, number:number + 1], slot.shape)
            found = jnp.take_along_axis(line, place, axis=1)
            result = jnp.where(row == number, found, result)
        out_ref[batch] = result


def body(ensemble, obs_values, obs_error_var, obs_lat, obs_lon, obs_level, obs_frac, loc_mask):
    members, var_count, level_dev, lat_dev, lon_dev = ensemble.shape
    batches, blocks = loc_mask.shape[:2]
    obs_total = obs_values.shape[1]
    lat_parts, lon_parts, lev_parts = (lax.axis_size(name) for name in AXES)
    lat_at, lon_at, lev_at = (lax.axis_index(name) for name in AXES)
    lon_total, level_total, lat_total = lon_dev * lon_parts, level_dev * lev_parts, lat_dev * lat_parts
    lat_start, lon_start, level_start = lat_at * lat_dev, lon_at * lon_dev, lev_at * level_dev
    slabs = var_count * level_dev * lat_dev
    keep = (lat_at * lon_parts + lon_at) % blocks

    variable, level = obs_level // level_total, obs_level % level_total
    level_local = level - level_start
    cells, slots = [], []
    for row_step, col_step in ((0, 0), (1, 0), (0, 1), (1, 1)):
        row = obs_lat + row_step
        col = (obs_lon + col_step) % lon_total
        row_local, col_local = row - lat_start, col - lon_start
        held = (
            (level_local >= 0) & (level_local < level_dev) & (row_local >= 0) & (row_local < lat_dev)
            & (col_local >= 0) & (col_local < lon_dev)
        )
        cell = ((variable * level_dev + level_local) * lat_dev + row_local) * lon_dev + col_local
        cells.append(jnp.where(held, cell, -1))
        slots.append((obs_level * lat_total + row) * lon_parts + col // lon_dev)
    cells = jnp.stack(cells)
    slots = jnp.stack([slot.reshape(batches, blocks, LANES) for slot in slots], axis=2)
    spots = jnp.where(jnp.max(cells, axis=0) >= 0, jnp.arange(obs_total, dtype=i32), obs_total)
    grid = spots.reshape(batches, blocks, LANES)
    lane = jnp.arange(LANES)
    inside = jnp.min(jnp.where(lane[:, None] <= lane, grid[:, :, None, :], obs_total), axis=3)
    number = jnp.arange(blocks)
    beyond = jnp.min(jnp.where(number[:, None] < number, jnp.min(grid, axis=2)[:, None, :], obs_total), axis=2)
    nxt = jnp.minimum(inside, beyond[:, :, None]).reshape(batches, obs_total)
    nxt = jnp.concatenate([nxt, jnp.full((batches, 1), obs_total, i32)], axis=1)

    own = loc_mask.reshape(batches, blocks, slabs)
    count = jnp.sum(own, axis=2)
    rank = jnp.cumsum(own, axis=2) - 1
    padded = slabs + CHUNK
    hit = (rank[..., None] == jnp.arange(padded)) & (own[..., None] > 0)
    number = jnp.arange(slabs, dtype=i32)[:, None]
    active = slabs + jnp.sum(jnp.where(hit, number - slabs, 0), axis=2)

    def rows_of(values):
        return values.astype(f32).reshape(batches, blocks, LANES)

    obs_rows = jnp.stack(
        [rows_of(v) for v in (obs_lat, obs_lon, obs_frac[:, 0], obs_frac[:, 1], obs_values, obs_error_var,
                              (obs_lon + 1) % lon_total, obs_lat)],
        axis=2,
    )
    devices, tiles = lat_parts * lon_parts * lev_parts, 4 * blocks
    carry = tiles // devices if batches == 2 and tiles % devices == 0 and 4 % (tiles // devices) == 0 else 0
    first = ((lev_at * lat_parts + lat_at) * lon_parts + lon_at) * carry
    where = jnp.stack([lat_start, lon_start, keep, first % 4]).astype(i32)

    def extended(values):
        ahead = lax.dynamic_index_in_dim(values[-1], first // 4, 0, True)
        more = jnp.concatenate([jnp.zeros_like(ahead), ahead], axis=0)
        return jnp.concatenate([values, jnp.broadcast_to(more, (batches,) + more.shape)], axis=1)

    obs_rows, slots = extended(obs_rows), extended(slots)
    smem = pl.BlockSpec(memory_space=pltpu.SMEM)
    vmem = pl.BlockSpec(memory_space=pltpu.VMEM)
    params = pltpu.CompilerParams(vmem_limit_bytes=56 * 1024 * 1024)
    state_shape = jax.ShapeDtypeStruct((slabs + 1, members, LANES), f32)
    natural_shape = jax.ShapeDtypeStruct((members, slabs, LANES), f32)

    def pick(which, x, natural):
        stencil_shape = jax.ShapeDtypeStruct((which.stop - which.start, blocks, 4, members, LANES), f32)
        return pl.pallas_call(
            pick_kernel,
            out_shape=(stencil_shape, state_shape) if natural else (stencil_shape,),
            in_specs=[smem, smem, vmem],
            out_specs=(vmem, vmem) if natural else (vmem,),
            compiler_params=params,
        )(nxt[which], cells[:, which], x)

    dims = (lat_dev, lon_dev, lon_total)

    def assimilate(batch, stencils):
        shapes = (
            jax.ShapeDtypeStruct((blocks, 2, LANES), f32),
            jax.ShapeDtypeStruct((2, LANES), f32),
            jax.ShapeDtypeStruct((blocks, LANES, 256), bf16),
            jax.ShapeDtypeStruct((blocks, 2 * members, 256), bf16),
        )
        return pl.pallas_call(
            functools.partial(stencil_kernel, dims),
            out_shape=shapes,
            in_specs=[smem] + [vmem] * 3,
            out_specs=(vmem,) * len(shapes),
            scratch_shapes=[
                pltpu.VMEM((blocks + 1, 4, members, LANES), f32),
                pltpu.VMEM((2, LANES, LANES), f32),
            ],
            compiler_params=params,
        )(where, obs_rows[batch], words[batch], stencils.reshape(blocks, 4, members, LANES))

    def bring(batch, share, factors):
        return pl.pallas_call(
            functools.partial(carry_kernel, dims),
            out_shape=jax.ShapeDtypeStruct((carry, members, LANES), f32),
            in_specs=[smem] + [vmem] * 5,
            out_specs=vmem,
            compiler_params=params,
        )(where, obs_rows[batch], words[batch], *factors, share.reshape(carry, members, LANES)).reshape(-1, LANES)

    def advance(batch, x, factors, span):
        last = batch == batches - 1 and span[1] == blocks
        return pl.pallas_call(
            functools.partial(own_kernel, dims, span, last),
            out_shape=natural_shape if last else state_shape,
            in_specs=[smem] * 3 + [vmem] * 4,
            out_specs=vmem,
            scratch_shapes=[pltpu.VMEM((lat_dev, LANES, LANES), f32)]
            + ([pltpu.VMEM(state_shape.shape, f32)] if last else []),
            compiler_params=params,
        )(where, count[batch], active[batch], obs_rows[batch], *factors, x)

    natural = ensemble.reshape(members, slabs, LANES)
    together = lax.optimization_barrier
    picked, x = pick(slice(0, 1), natural, True)
    share = share_sum(picked.reshape(1, -1, LANES), "lev")
    if carry:
        share, x = together((share, x))
        ahead = pick(slice(1, 2), x, False)[0].reshape(1, -1, LANES)
    share = share_sum(share, "lat")
    masks = loc_mask.reshape(batches * blocks, slabs)
    if carry:
        share, ahead, masks = together((share, ahead, masks))
        ahead = share_sum(ahead, "lev")
    share = share_sum(share, "lon")[0]
    masks = collect(masks, "lon")
    share, masks = together((share, masks))
    stencils = collect(share, "lon").reshape(-1, LANES)
    masks = collect(masks, "lat")
    stencils, masks = together((stencils, masks))
    stencils = collect(stencils, "lat").reshape(-1, LANES)
    masks = collect(masks, "lev").reshape(lev_parts, lat_parts, lon_parts, batches, blocks, slabs)
    bits = together(jnp.sum(masks << jnp.arange(blocks, dtype=i32)[:, None], axis=4))
    bits = bits.reshape(lev_parts, lat_parts, lon_parts, batches, var_count, level_dev, lat_dev)
    bits = bits.transpose(3, 4, 0, 5, 1, 6, 2).reshape(batches, -1)
    bits = jnp.pad(bits, ((0, 0), (0, -bits.shape[1] % LANES))).reshape(batches, -1, LANES)
    words = pl.pallas_call(
        word_kernel,
        out_shape=jax.ShapeDtypeStruct((batches, (blocks + 2) * 4, LANES), i32),
        in_specs=[vmem, vmem],
        out_specs=vmem,
    )(slots.reshape(batches, -1, LANES), bits).reshape(batches, blocks + 2, 4, LANES)
    if carry:
        stencils, ahead, words = together((stencils, ahead, words))
    stencils = collect(stencils, "lev")
    if carry:
        stencils, ahead = together((stencils, ahead))
    prior_parts, post_parts = [], []
    for batch in range(batches):
        prior, post, *factors = assimilate(batch, stencils)
        prior_parts.append(prior.transpose(1, 0, 2).reshape(2, obs_total))
        post_parts.append(post)
        if batch == batches - 1:
            rows, names, cuts = jnp.concatenate(post_parts, axis=0), ("lon", "lat"), (0, blocks // 2, blocks)
        elif carry:
            ahead = share_sum(ahead, "lat")
            ahead, factors = together((ahead, factors))
            ahead = share_sum(ahead, "lon")
            x = advance(batch, x, factors, (0, blocks // 4))
            ahead, x = together((ahead, x))
            rows = bring(batch, ahead, factors)
            names, cuts = ("lon", "lat", "lev"), (blocks // 4, blocks * 7 // 16, blocks * 7 // 8, blocks)
        else:
            x = advance(batch, x, factors, (0, blocks))
            stencils = whole_of(share_of(pick(slice(batch + 1, batch + 2), x, False)[0])[0])
            continue
        for name, start, stop in zip(names, cuts, cuts[1:]):
            rows = collect(rows, name).reshape(-1, LANES)
            x = advance(batch, x, factors, (start, stop))
            rows, x = together((rows, x))
        stencils = rows
    posts = stencils.reshape(-1, 2 * batches, LANES)[:blocks]
    posts = posts.transpose(1, 0, 2).reshape(batches, 2, obs_total)
    return x.reshape(ensemble.shape), jnp.stack(prior_parts), posts


def solution(mesh):
    state = P(None, None, "lev", "lat", "lon")
    return jax.shard_map(
        body,
        mesh=mesh,
        in_specs=(state, P(), P(), P(), P(), P(), P(), P(None, None, None, "lev", "lat", "lon")),
        out_specs=(state, P(), P()),
        check_vma=False,
    )
```

```python
import functools

import jax
import jax.numpy as jnp
from jax import lax
from jax.experimental import pallas as pl
from jax.experimental.pallas import tpu as pltpu
from jax.sharding import PartitionSpec as P

epsilon = 1e-06
AXES = ("lat", "lon", "lev")
LANES = 128
CHUNK = 20
HALF_LOG2E = 0.7213475204444817
GROUP = 3
PICKS = 2
f32, bf16, i32 = jnp.float32, jnp.bfloat16, jnp.int32


def split(values):
    high = values.astype(bf16)
    return high, (values - high.astype(f32)).astype(bf16)


def shifted(values, name, by):
    size = lax.axis_size(name)
    return lax.ppermute(values, name, [(i, (i + by) % size) for i in range(size)])


def share_sum(values, name):
    size, me = lax.axis_size(name), lax.axis_index(name)
    parts = values.reshape(values.shape[0], size, -1, LANES)
    total = lax.dynamic_index_in_dim(parts, me, 1, False)
    for by in range(1, size):
        total = total + shifted(lax.dynamic_index_in_dim(parts, (me + by) % size, 1, False), name, by)
    return total


def collect(values, name):
    size, me = lax.axis_size(name), lax.axis_index(name)
    result = jnp.zeros((size,) + values.shape, values.dtype)
    result = lax.dynamic_update_index_in_dim(result, values, me, 0)
    for by in range(1, size):
        result = lax.dynamic_update_index_in_dim(result, shifted(values, name, by), (me - by) % size, 0)
    return result


def pieces(values, name):
    return [values] + [shifted(values, name, by) for by in range(1, lax.axis_size(name))]


def share_of(values):
    rows = values.reshape(values.shape[0], -1, LANES)
    for name in ("lev", "lat", "lon"):
        rows = share_sum(rows, name)
    return rows


def whole_of(share):
    for name in ("lon", "lat", "lev"):
        share = collect(share, name).reshape(-1, LANES)
    return share


def pick_kernel(nxt_ref, idx_ref, x_ref, e_ref, *moved_ref):
    members = e_ref.shape[3]
    batches, obs_total = idx_ref.shape[1:]
    lane = lax.broadcasted_iota(i32, (members, LANES), 1)
    if moved_ref:
        source = moved_ref[0]
        for slab in range(x_ref.shape[1]):
            source[slab] = x_ref[:, slab, :]
        source[x_ref.shape[1]] = jnp.zeros((members, LANES), f32)
    else:
        source = x_ref
    e_ref[...] = jnp.zeros_like(e_ref)

    for batch in range(batches):
        def step(i):
            turned, put, spots = [], [], []
            for _ in range(PICKS):
                now = jnp.minimum(i, obs_total - 1)
                block, column = now // LANES, now % LANES
                for corner in range(4):
                    cell = idx_ref[corner, batch, now]
                    safe = jnp.maximum(cell, 0)
                    turned.append(pltpu.roll(source[safe // LANES], (column - safe % LANES + LANES) % LANES, 1))
                    put.append((lane == column) & (cell >= 0))
                    spots.append((block, corner))
                i = nxt_ref[batch, jnp.minimum(i + 1, obs_total)]
            for (block, corner), value, mask in zip(spots, turned, put):
                pltpu.store(e_ref.at[batch, block, corner], value, mask=mask)
            return i

        lax.while_loop(lambda i: i < obs_total, step, nxt_ref[batch, 0])


def lat_taper(rows, at, scale):
    gap = rows * scale - at
    return jnp.exp2(-(gap * gap))


def lon_taper(columns, at, scale, total):
    gap = jnp.abs(columns * scale - at)
    gap = jnp.minimum(gap, total * scale - gap)
    return jnp.exp2(-(gap * gap))


def scales(dims):
    return HALF_LOG2E**0.5 / dims[0], HALF_LOG2E**0.5 / (0.5 * dims[1])


def spread(row, scale):
    return jnp.broadcast_to(row * scale, (LANES, LANES)).T


def update(lhs1, lhs2, tiles, locality, bit=None):
    members = tiles[0].shape[0]
    pad = jnp.zeros((256 - 3 * members, LANES), bf16)
    columns = []
    for tile in tiles:
        high, low = split(tile)
        columns.append(jnp.concatenate([high, high, low, pad], axis=0))
    cov = jnp.dot(lhs1, jnp.concatenate(columns, axis=1), preferred_element_type=f32)
    columns = []
    for number in range(len(tiles)):
        gain = cov[:, number * LANES:(number + 1) * LANES] * locality(number)
        columns.append(jnp.concatenate(split(gain), axis=0))
    moved = jnp.dot(lhs2, jnp.concatenate(columns, axis=1), preferred_element_type=f32)
    results = []
    for number, tile in enumerate(tiles):
        lanes = slice(number * LANES, (number + 1) * LANES)
        change = moved[:members, lanes] + moved[members:, lanes]
        results.append(tile + (change if bit is None else change * bit(number)))
    return results


def stencil_kernel(dims, parts, where_ref, obs_ref, word_ref, *refs):
    lat_scale, lon_scale = scales(dims)
    lon_total = dims[2]
    e_in, (prior_ref, post_ref, lhs1_ref, lhs2_ref, e_ref, pos_ref) = refs[:-6], refs[-6:]
    blocks, members = prior_ref.shape[0], e_ref.shape[2]
    keep = where_ref[2]
    if parts:
        lat_parts, lon_parts, lev_parts = parts
        carried = e_in[0].shape[1]

        def place(step, c):
            lat_back, lon_back = step // lon_parts, step % lon_parts
            lat = (where_ref[4] - lat_back + lat_parts) % lat_parts
            lon = (where_ref[5] - lon_back + lon_parts) % lon_parts
            for lev_back in range(lev_parts):
                lev = (where_ref[6] - lev_back + lev_parts) % lev_parts
                for number in range(carried):
                    tile = ((lev * lat_parts + lat) * lon_parts + lon) * carried + number
                    e_ref[tile // 4, tile % 4] = e_in[lev_back][step, number]
            return c

        lax.fori_loop(0, lat_parts * lon_parts, place, 0)
    else:
        e_ref[0:blocks] = e_in[0][...]
    e_ref[blocks] = jnp.zeros((4, members, LANES), f32)
    pad_rows = 256 - 3 * members

    def observe(block):
        row = obs_ref[block]
        p, q = row[2:3], row[3:4]
        result = (1.0 - p) * (1.0 - q) * e_ref[block, 0]
        result = result + p * (1.0 - q) * e_ref[block, 1]
        result = result + (1.0 - p) * q * e_ref[block, 2]
        result = result + p * q * e_ref[block, 3]
        center = jnp.sum(result, axis=0, keepdims=True) / members
        anomaly = result - center
        variance = jnp.sum(anomaly * anomaly, axis=0, keepdims=True) / (members - 1) + epsilon
        return row, result, center, anomaly, variance

    def group_of(block, number):
        later = block + 1 + number
        end = jnp.where((later == blocks) & (keep <= block), keep, blocks)
        return jnp.where(later < blocks, later, end)

    def assimilate(block, carry):
        row, result, center, anomaly, variance = observe(block)
        y, r = row[4:5], row[5:6]
        denominator = variance + r
        post_mean = (center * r + y * variance) / denominator
        increment = post_mean + jnp.sqrt(r / denominator) * anomaly - result
        prior_ref[block] = jnp.concatenate([center, jnp.sqrt(variance)], axis=0)
        scaled = increment / (variance * (members - 1))
        r_high, r_low = split(scaled)
        lhs2_ref[block] = jnp.concatenate(
            [
                jnp.concatenate([r_high, r_high], axis=1),
                jnp.concatenate([r_low, jnp.zeros_like(r_low)], axis=1),
            ],
            axis=0,
        )
        d_high = anomaly.astype(bf16).astype(f32)
        d_low = anomaly - d_high
        packed = jnp.concatenate([d_high, d_low, d_high, jnp.zeros((pad_rows, LANES), f32)], axis=0)
        lhs1_ref[block] = packed.T.astype(bf16)
        pos_ref[0] = spread(row[0:1] + row[2:3], lat_scale)
        pos_ref[1] = spread(row[1:2] + row[3:4], lon_scale)

        def stencil(step, c):
            others = [group_of(block, step * GROUP + number) for number in range(GROUP)]
            la, lo = pos_ref[0], pos_ref[1]
            lats, lons, bits = [], [], []
            for other in others:
                orow = obs_ref[other]
                lats.append([lat_taper(orow[0:1], la, lat_scale), lat_taper(orow[0:1] + 1.0, la, lat_scale)])
                lons.append([lon_taper(orow[at:at + 1], lo, lon_scale, lon_total) for at in (1, 6)])
                bits.append(((word_ref[other] >> block) & 1).astype(f32))

            def locality(number):
                which, corner = number // 4, number % 4
                return lats[which][corner % 2] * lons[which][corner // 2]

            def bit(number):
                return bits[number // 4][number % 4:number % 4 + 1]

            tiles = [e_ref[other, corner] for other in others for corner in range(4)]
            for number, tile in enumerate(update(lhs1_ref[block], lhs2_ref[block], tiles, locality, bit)):
                e_ref[others[number // 4], number % 4] = tile
            return c

        pending = blocks - 1 - block + (keep <= block).astype(i32)
        lax.fori_loop(0, pl.cdiv(pending, GROUP), stencil, 0)
        return carry

    lax.fori_loop(0, blocks, assimilate, 0)
    row, result, center, anomaly, variance = observe(keep)
    post_ref[...] = jnp.concatenate([center, jnp.sqrt(variance)], axis=0)


def carry_kernel(dims, where_ref, obs_ref, word_ref, lhs1_ref, lhs2_ref, in_ref, out_ref):
    lat_scale, lon_scale = scales(dims)
    blocks, first = lhs1_ref.shape[0], where_ref[3]
    out_ref[...] = in_ref[...]
    orow, words = obs_ref[blocks + 1], word_ref[blocks + 1]
    rows, columns, masks = [], [], []
    for number in range(in_ref.shape[0]):
        corner = first + number
        rows.append(orow[0:1] + (corner % 2).astype(f32))
        columns.append(jnp.where(corner // 2 == 0, orow[1:2], orow[6:7]))
        masks.append(sum(jnp.where(corner == c, words[c:c + 1], 0) for c in range(4)))

    def assimilate(block):
        row = obs_ref[block]
        lat_at = spread(row[0:1] + row[2:3], lat_scale)
        lon_at = spread(row[1:2] + row[3:4], lon_scale)
        near = [lat_taper(r, lat_at, lat_scale) * lon_taper(c, lon_at, lon_scale, dims[2]) for r, c in zip(rows, columns)]
        bits = [((mask >> block) & 1).astype(f32) for mask in masks]
        tiles = [out_ref[number] for number in range(len(rows))]
        new = update(lhs1_ref[block], lhs2_ref[block], tiles, lambda n: near[n], lambda n: bits[n])
        for number, tile in enumerate(new):
            out_ref[number] = tile

    def several(step, c):
        for number in range(4):
            assimilate(step * 4 + number)
        return c

    lax.fori_loop(0, blocks // 4, several, 0)


def own_kernel(dims, span, last, where_ref, count_ref, list_ref, obs_ref, lhs1_ref, lhs2_ref, x_ref, out_ref, loc_ref, *scratch):
    lat_scale, lon_scale = scales(dims)
    lat_dev, lon_dev, lon_total = dims
    lat_start, lon_start = where_ref[0], where_ref[1]
    state = scratch[0] if last else out_ref
    state[...] = x_ref[...]
    columns = (lon_start + lax.broadcasted_iota(i32, (LANES, LANES), 1)).astype(f32)

    def assimilate(block, carry):
        row = obs_ref[block]
        lat_at = spread(row[0:1] + row[2:3], lat_scale)
        own_lon = lon_taper(columns, spread(row[1:2] + row[3:4], lon_scale), lon_scale, lon_total)
        for a in range(lat_dev):
            loc_ref[a] = lat_taper((lat_start + a).astype(f32), lat_at, lat_scale) * own_lon

        def own(step, c):
            which = [list_ref[block, step * CHUNK + number] for number in range(CHUNK)]
            new = update(lhs1_ref[block], lhs2_ref[block], [state[w] for w in which],
                         lambda number: loc_ref[which[number] % lat_dev])
            for number in range(CHUNK):
                state[which[number]] = new[number]
            return c

        lax.fori_loop(0, pl.cdiv(count_ref[block], CHUNK), own, 0)
        return carry

    lax.fori_loop(span[0], span[1], assimilate, 0)
    if last:
        for slab in range(out_ref.shape[1]):
            out_ref[:, slab, :] = state[slab]


def word_kernel(slot_ref, table_ref, out_ref):
    for batch in range(slot_ref.shape[0]):
        slot = slot_ref[batch]
        place = slot % LANES
        row = slot // LANES
        result = jnp.zeros_like(slot)
        for number in range(table_ref.shape[1]):
            line = jnp.broadcast_to(table_ref[batch, number:number + 1], slot.shape)
            found = jnp.take_along_axis(line, place, axis=1)
            result = jnp.where(row == number, found, result)
        out_ref[batch] = result


def body(ensemble, obs_values, obs_error_var, obs_lat, obs_lon, obs_level, obs_frac, loc_mask):
    members, var_count, level_dev, lat_dev, lon_dev = ensemble.shape
    batches, blocks = loc_mask.shape[:2]
    obs_total = obs_values.shape[1]
    lat_parts, lon_parts, lev_parts = (lax.axis_size(name) for name in AXES)
    lat_at, lon_at, lev_at = (lax.axis_index(name) for name in AXES)
    lon_total, level_total, lat_total = lon_dev * lon_parts, level_dev * lev_parts, lat_dev * lat_parts
    lat_start, lon_start, level_start = lat_at * lat_dev, lon_at * lon_dev, lev_at * level_dev
    slabs = var_count * level_dev * lat_dev
    keep = (lat_at * lon_parts + lon_at) % blocks

    variable, level = obs_level // level_total, obs_level % level_total
    level_local = level - level_start
    cells, slots = [], []
    for row_step, col_step in ((0, 0), (1, 0), (0, 1), (1, 1)):
        row = obs_lat + row_step
        col = (obs_lon + col_step) % lon_total
        row_local, col_local = row - lat_start, col - lon_start
        held = (
            (level_local >= 0) & (level_local < level_dev) & (row_local >= 0) & (row_local < lat_dev)
            & (col_local >= 0) & (col_local < lon_dev)
        )
        cell = ((variable * level_dev + level_local) * lat_dev + row_local) * lon_dev + col_local
        cells.append(jnp.where(held, cell, -1))
        slots.append((obs_level * lat_total + row) * lon_parts + col // lon_dev)
    cells = jnp.stack(cells)
    slots = jnp.stack([slot.reshape(batches, blocks, LANES) for slot in slots], axis=2)
    spots = jnp.where(jnp.max(cells, axis=0) >= 0, jnp.arange(obs_total, dtype=i32), obs_total)
    grid = spots.reshape(batches, blocks, LANES)
    lane = jnp.arange(LANES)
    inside = jnp.min(jnp.where(lane[:, None] <= lane, grid[:, :, None, :], obs_total), axis=3)
    number = jnp.arange(blocks)
    beyond = jnp.min(jnp.where(number[:, None] < number, jnp.min(grid, axis=2)[:, None, :], obs_total), axis=2)
    nxt = jnp.minimum(inside, beyond[:, :, None]).reshape(batches, obs_total)
    nxt = jnp.concatenate([nxt, jnp.full((batches, 1), obs_total, i32)], axis=1)

    own = loc_mask.reshape(batches, blocks, slabs)
    count = jnp.sum(own, axis=2)
    rank = jnp.cumsum(own, axis=2) - 1
    padded = slabs + CHUNK
    hit = (rank[..., None] == jnp.arange(padded)) & (own[..., None] > 0)
    number = jnp.arange(slabs, dtype=i32)[:, None]
    active = slabs + jnp.sum(jnp.where(hit, number - slabs, 0), axis=2)

    def rows_of(values):
        return values.astype(f32).reshape(batches, blocks, LANES)

    obs_rows = jnp.stack(
        [rows_of(v) for v in (obs_lat, obs_lon, obs_frac[:, 0], obs_frac[:, 1], obs_values, obs_error_var,
                              (obs_lon + 1) % lon_total, obs_lat)],
        axis=2,
    )
    devices, tiles = lat_parts * lon_parts * lev_parts, 4 * blocks
    carry = tiles // devices if batches == 2 and tiles % devices == 0 and 4 % (tiles // devices) == 0 else 0
    first = ((lev_at * lat_parts + lat_at) * lon_parts + lon_at) * carry
    where = jnp.stack([lat_start, lon_start, keep, first % 4, lat_at, lon_at, lev_at]).astype(i32)

    def extended(values):
        ahead = lax.dynamic_index_in_dim(values[-1], first // 4, 0, True)
        more = jnp.concatenate([jnp.zeros_like(ahead), ahead], axis=0)
        return jnp.concatenate([values, jnp.broadcast_to(more, (batches,) + more.shape)], axis=1)

    obs_rows, slots = extended(obs_rows), extended(slots)
    smem = pl.BlockSpec(memory_space=pltpu.SMEM)
    vmem = pl.BlockSpec(memory_space=pltpu.VMEM)
    params = pltpu.CompilerParams(vmem_limit_bytes=56 * 1024 * 1024)
    state_shape = jax.ShapeDtypeStruct((slabs + 1, members, LANES), f32)
    natural_shape = jax.ShapeDtypeStruct((members, slabs, LANES), f32)

    def pick(which, x, natural):
        stencil_shape = jax.ShapeDtypeStruct((which.stop - which.start, blocks, 4, members, LANES), f32)
        return pl.pallas_call(
            pick_kernel,
            out_shape=(stencil_shape, state_shape) if natural else (stencil_shape,),
            in_specs=[smem, smem, vmem],
            out_specs=(vmem, vmem) if natural else (vmem,),
            compiler_params=params,
        )(nxt[which], cells[:, which], x)

    dims = (lat_dev, lon_dev, lon_total)

    def assimilate(batch, stencils):
        shapes = (
            jax.ShapeDtypeStruct((blocks, 2, LANES), f32),
            jax.ShapeDtypeStruct((2, LANES), f32),
            jax.ShapeDtypeStruct((blocks, LANES, 256), bf16),
            jax.ShapeDtypeStruct((blocks, 2 * members, 256), bf16),
        )
        return pl.pallas_call(
            functools.partial(stencil_kernel, dims, (lat_parts, lon_parts, lev_parts) if carry else None),
            out_shape=shapes,
            in_specs=[smem] + [vmem] * (2 + len(stencils)),
            out_specs=(vmem,) * len(shapes),
            scratch_shapes=[
                pltpu.VMEM((blocks + 1, 4, members, LANES), f32),
                pltpu.VMEM((2, LANES, LANES), f32),
            ],
            compiler_params=params,
        )(where, obs_rows[batch], words[batch], *stencils)

    def shaped(stencils):
        if carry:
            return [part.reshape(lat_parts * lon_parts, carry, members, LANES) for part in stencils]
        return [stencils.reshape(blocks, 4, members, LANES)]

    def gathered(rows, name):
        if not carry:
            return collect(rows, name).reshape(-1, LANES)
        return pieces(rows, name) if name == "lev" else jnp.concatenate(pieces(rows, name), axis=0)

    def bring(batch, share, factors):
        return pl.pallas_call(
            functools.partial(carry_kernel, dims),
            out_shape=jax.ShapeDtypeStruct((carry, members, LANES), f32),
            in_specs=[smem] + [vmem] * 5,
            out_specs=vmem,
            compiler_params=params,
        )(where, obs_rows[batch], words[batch], *factors, share.reshape(carry, members, LANES)).reshape(-1, LANES)

    def advance(batch, x, factors, span):
        last = batch == batches - 1 and span[1] == blocks
        return pl.pallas_call(
            functools.partial(own_kernel, dims, span, last),
            out_shape=natural_shape if last else state_shape,
            in_specs=[smem] * 3 + [vmem] * 4,
            out_specs=vmem,
            scratch_shapes=[pltpu.VMEM((lat_dev, LANES, LANES), f32)]
            + ([pltpu.VMEM(state_shape.shape, f32)] if last else []),
            compiler_params=params,
        )(where, count[batch], active[batch], obs_rows[batch], *factors, x)

    natural = ensemble.reshape(members, slabs, LANES)
    together = lax.optimization_barrier
    picked, x = pick(slice(0, 1), natural, True)
    share = share_sum(picked.reshape(1, -1, LANES), "lev")
    if carry:
        share, x = together((share, x))
        ahead = pick(slice(1, 2), x, False)[0].reshape(1, -1, LANES)
    share = share_sum(share, "lat")
    masks = loc_mask.reshape(batches * blocks, slabs)
    if carry:
        share, ahead, masks = together((share, ahead, masks))
        ahead = share_sum(ahead, "lev")
    share = share_sum(share, "lon")[0]
    masks = collect(masks, "lon")
    share, masks = together((share, masks))
    stencils = gathered(share, "lon")
    masks = collect(masks, "lat")
    stencils, masks = together((stencils, masks))
    stencils = gathered(stencils, "lat")
    masks = collect(masks, "lev").reshape(lev_parts, lat_parts, lon_parts, batches, blocks, slabs)
    bits = together(jnp.sum(masks << jnp.arange(blocks, dtype=i32)[:, None], axis=4))
    bits = bits.reshape(lev_parts, lat_parts, lon_parts, batches, var_count, level_dev, lat_dev)
    bits = bits.transpose(3, 4, 0, 5, 1, 6, 2).reshape(batches, -1)
    bits = jnp.pad(bits, ((0, 0), (0, -bits.shape[1] % LANES))).reshape(batches, -1, LANES)
    words = pl.pallas_call(
        word_kernel,
        out_shape=jax.ShapeDtypeStruct((batches, (blocks + 2) * 4, LANES), i32),
        in_specs=[vmem, vmem],
        out_specs=vmem,
    )(slots.reshape(batches, -1, LANES), bits).reshape(batches, blocks + 2, 4, LANES)
    if carry:
        stencils, ahead, words = together((stencils, ahead, words))
    stencils = gathered(stencils, "lev")
    if carry:
        stencils, ahead = together((stencils, ahead))
    prior_parts, post_parts = [], []
    for batch in range(batches):
        prior, post, *factors = assimilate(batch, shaped(stencils))
        prior_parts.append(prior.transpose(1, 0, 2).reshape(2, obs_total))
        post_parts.append(post)
        if batch == batches - 1:
            rows, names, cuts = jnp.concatenate(post_parts, axis=0), ("lon", "lat"), (0, blocks // 2, blocks)
        elif carry:
            ahead = share_sum(ahead, "lat")
            ahead, factors = together((ahead, factors))
            ahead = share_sum(ahead, "lon")
            x = advance(batch, x, factors, (0, blocks // 4))
            ahead, x = together((ahead, x))
            rows = bring(batch, ahead, factors)
            names, cuts = ("lon", "lat", "lev"), (blocks // 4, blocks * 7 // 16, blocks * 7 // 8, blocks)
        else:
            x = advance(batch, x, factors, (0, blocks))
            stencils = whole_of(share_of(pick(slice(batch + 1, batch + 2), x, False)[0])[0])
            continue
        for name, start, stop in zip(names, cuts, cuts[1:]):
            if batch == batches - 1:
                rows = collect(rows, name).reshape(-1, LANES)
            else:
                rows = gathered(rows, name)
            x = advance(batch, x, factors, (start, stop))
            rows, x = together((rows, x))
        stencils = rows
    posts = stencils.reshape(-1, 2 * batches, LANES)[:blocks]
    posts = posts.transpose(1, 0, 2).reshape(batches, 2, obs_total)
    return x.reshape(ensemble.shape), jnp.stack(prior_parts), posts


def solution(mesh):
    state = P(None, None, "lev", "lat", "lon")
    return jax.shard_map(
        body,
        mesh=mesh,
        in_specs=(state, P(), P(), P(), P(), P(), P(), P(None, None, None, "lev", "lat", "lon")),
        out_specs=(state, P(), P()),
        check_vma=False,
    )
```

```python
import functools

import jax
import jax.numpy as jnp
from jax import lax
from jax.experimental import pallas as pl
from jax.experimental.pallas import tpu as pltpu
from jax.sharding import PartitionSpec as P

epsilon = 1e-06
AXES = ("lat", "lon", "lev")
LANES = 128
CHUNK = 20
HALF_LOG2E = 0.7213475204444817
GROUP = 3
PICKS = 2
f32, bf16, i32 = jnp.float32, jnp.bfloat16, jnp.int32


def split(values):
    high = values.astype(bf16)
    return high, (values - high.astype(f32)).astype(bf16)


def shifted(values, name, by):
    size = lax.axis_size(name)
    return lax.ppermute(values, name, [(i, (i + by) % size) for i in range(size)])


def share_sum(values, name):
    size, me = lax.axis_size(name), lax.axis_index(name)
    parts = values.reshape(values.shape[0], size, -1, LANES)
    total = lax.dynamic_index_in_dim(parts, me, 1, False)
    for by in range(1, size):
        total = total + shifted(lax.dynamic_index_in_dim(parts, (me + by) % size, 1, False), name, by)
    return total


def collect(values, name):
    size, me = lax.axis_size(name), lax.axis_index(name)
    result = jnp.zeros((size,) + values.shape, values.dtype)
    result = lax.dynamic_update_index_in_dim(result, values, me, 0)
    for by in range(1, size):
        result = lax.dynamic_update_index_in_dim(result, shifted(values, name, by), (me - by) % size, 0)
    return result


def pieces(values, name):
    return [values] + [shifted(values, name, by) for by in range(1, lax.axis_size(name))]


def share_of(values):
    rows = values.reshape(values.shape[0], -1, LANES)
    for name in ("lev", "lat", "lon"):
        rows = share_sum(rows, name)
    return rows


def whole_of(share):
    for name in ("lon", "lat", "lev"):
        share = collect(share, name).reshape(-1, LANES)
    return share


def pick_kernel(nxt_ref, idx_ref, x_ref, e_ref, *moved_ref):
    members = e_ref.shape[3]
    batches, obs_total = idx_ref.shape[1:]
    lane = lax.broadcasted_iota(i32, (members, LANES), 1)
    if moved_ref:
        source = moved_ref[0]
        for slab in range(x_ref.shape[1]):
            source[slab] = x_ref[:, slab, :]
        source[x_ref.shape[1]] = jnp.zeros((members, LANES), f32)
    else:
        source = x_ref
    e_ref[...] = jnp.zeros_like(e_ref)

    for batch in range(batches):
        def step(i):
            turned, put, spots = [], [], []
            for _ in range(PICKS):
                now = jnp.minimum(i, obs_total - 1)
                block, column = now // LANES, now % LANES
                for corner in range(4):
                    cell = idx_ref[corner, batch, now]
                    safe = jnp.maximum(cell, 0)
                    turned.append(pltpu.roll(source[safe // LANES], (column - safe % LANES + LANES) % LANES, 1))
                    put.append((lane == column) & (cell >= 0))
                    spots.append((block, corner))
                i = nxt_ref[batch, jnp.minimum(i + 1, obs_total)]
            for (block, corner), value, mask in zip(spots, turned, put):
                pltpu.store(e_ref.at[batch, block, corner], value, mask=mask)
            return i

        lax.while_loop(lambda i: i < obs_total, step, nxt_ref[batch, 0])


def lat_taper(rows, at, scale):
    gap = rows * scale - at
    return jnp.exp2(-(gap * gap))


def lon_taper(columns, at, scale, total):
    gap = jnp.abs(columns * scale - at)
    gap = jnp.minimum(gap, total * scale - gap)
    return jnp.exp2(-(gap * gap))


def scales(dims):
    return HALF_LOG2E**0.5 / dims[0], HALF_LOG2E**0.5 / (0.5 * dims[1])


def spread(row, scale):
    return jnp.broadcast_to(row * scale, (LANES, LANES)).T


def update(lhs1, lhs2, tiles, locality, bit=None):
    members = tiles[0].shape[0]
    pad = jnp.zeros((256 - 3 * members, LANES), bf16)
    columns = []
    for tile in tiles:
        high, low = split(tile)
        columns.append(jnp.concatenate([high, high, low, pad], axis=0))
    cov = jnp.dot(lhs1, jnp.concatenate(columns, axis=1), preferred_element_type=f32)
    columns = []
    for number in range(len(tiles)):
        gain = cov[:, number * LANES:(number + 1) * LANES] * locality(number)
        columns.append(jnp.concatenate(split(gain), axis=0))
    moved = jnp.dot(lhs2, jnp.concatenate(columns, axis=1), preferred_element_type=f32)
    results = []
    for number, tile in enumerate(tiles):
        lanes = slice(number * LANES, (number + 1) * LANES)
        change = moved[:members, lanes] + moved[members:, lanes]
        results.append(tile + (change if bit is None else change * bit(number)))
    return results


def stencil_kernel(dims, parts, where_ref, obs_ref, word_ref, *refs):
    lat_scale, lon_scale = scales(dims)
    lon_total = dims[2]
    e_in, (prior_ref, post_ref, lhs1_ref, lhs2_ref, e_ref, pos_ref) = refs[:-6], refs[-6:]
    blocks, members = prior_ref.shape[0], e_ref.shape[2]
    keep = where_ref[2]
    if parts:
        lat_parts, lon_parts, lev_parts = parts
        carried = e_in[0].shape[1]

        def place(step, c):
            lat_back, lon_back = step // lon_parts, step % lon_parts
            lat = (where_ref[4] - lat_back + lat_parts) % lat_parts
            lon = (where_ref[5] - lon_back + lon_parts) % lon_parts
            for lev_back in range(lev_parts):
                lev = (where_ref[6] - lev_back + lev_parts) % lev_parts
                for number in range(carried):
                    tile = ((lev * lat_parts + lat) * lon_parts + lon) * carried + number
                    e_ref[tile // 4, tile % 4] = e_in[lev_back][step, number]
            return c

        lax.fori_loop(0, lat_parts * lon_parts, place, 0)
    else:
        e_ref[0:blocks] = e_in[0][...]
    e_ref[blocks] = jnp.zeros((4, members, LANES), f32)
    pad_rows = 256 - 3 * members

    def observe(block):
        row = obs_ref[block]
        p, q = row[2:3], row[3:4]
        result = (1.0 - p) * (1.0 - q) * e_ref[block, 0]
        result = result + p * (1.0 - q) * e_ref[block, 1]
        result = result + (1.0 - p) * q * e_ref[block, 2]
        result = result + p * q * e_ref[block, 3]
        center = jnp.sum(result, axis=0, keepdims=True) / members
        anomaly = result - center
        variance = jnp.sum(anomaly * anomaly, axis=0, keepdims=True) / (members - 1) + epsilon
        return row, result, center, anomaly, variance

    def group_of(block, number):
        later = block + 1 + number
        end = jnp.where((later == blocks) & (keep <= block), keep, blocks)
        return jnp.where(later < blocks, later, end)

    def assimilate(block, carry):
        row, result, center, anomaly, variance = observe(block)
        y, r = row[4:5], row[5:6]
        denominator = variance + r
        post_mean = (center * r + y * variance) / denominator
        increment = post_mean + jnp.sqrt(r / denominator) * anomaly - result
        prior_ref[block] = jnp.concatenate([center, jnp.sqrt(variance)], axis=0)
        scaled = increment / (variance * (members - 1))
        r_high, r_low = split(scaled)
        lhs2_ref[block] = jnp.concatenate(
            [
                jnp.concatenate([r_high, r_high], axis=1),
                jnp.concatenate([r_low, jnp.zeros_like(r_low)], axis=1),
            ],
            axis=0,
        )
        d_high = anomaly.astype(bf16).astype(f32)
        d_low = anomaly - d_high
        packed = jnp.concatenate([d_high, d_low, d_high, jnp.zeros((pad_rows, LANES), f32)], axis=0)
        lhs1_ref[block] = packed.T.astype(bf16)
        pos_ref[0] = spread(row[0:1] + row[2:3], lat_scale)
        pos_ref[1] = spread(row[1:2] + row[3:4], lon_scale)

        def stencil(step, c):
            others = [group_of(block, step * GROUP + number) for number in range(GROUP)]
            la, lo = pos_ref[0], pos_ref[1]
            lats, lons, bits = [], [], []
            for other in others:
                orow = obs_ref[other]
                lats.append([lat_taper(orow[0:1], la, lat_scale), lat_taper(orow[0:1] + 1.0, la, lat_scale)])
                lons.append([lon_taper(orow[at:at + 1], lo, lon_scale, lon_total) for at in (1, 6)])
                bits.append(((word_ref[other] >> block) & 1).astype(f32))

            def locality(number):
                which, corner = number // 4, number % 4
                return lats[which][corner % 2] * lons[which][corner // 2]

            def bit(number):
                return bits[number // 4][number % 4:number % 4 + 1]

            tiles = [e_ref[other, corner] for other in others for corner in range(4)]
            for number, tile in enumerate(update(lhs1_ref[block], lhs2_ref[block], tiles, locality, bit)):
                e_ref[others[number // 4], number % 4] = tile
            return c

        pending = blocks - 1 - block + (keep <= block).astype(i32)
        lax.fori_loop(0, pl.cdiv(pending, GROUP), stencil, 0)
        return carry

    lax.fori_loop(0, blocks, assimilate, 0)
    row, result, center, anomaly, variance = observe(keep)
    post_ref[...] = jnp.concatenate([center, jnp.sqrt(variance)], axis=0)


def carry_kernel(dims, where_ref, obs_ref, word_ref, lhs1_ref, lhs2_ref, in_ref, out_ref):
    lat_scale, lon_scale = scales(dims)
    blocks, first = lhs1_ref.shape[0], where_ref[3]
    out_ref[...] = in_ref[...]
    orow, words = obs_ref[blocks + 1], word_ref[blocks + 1]
    rows, columns, masks = [], [], []
    for number in range(in_ref.shape[0]):
        corner = first + number
        rows.append(orow[0:1] + (corner % 2).astype(f32))
        columns.append(jnp.where(corner // 2 == 0, orow[1:2], orow[6:7]))
        masks.append(sum(jnp.where(corner == c, words[c:c + 1], 0) for c in range(4)))

    def assimilate(block):
        row = obs_ref[block]
        lat_at = spread(row[0:1] + row[2:3], lat_scale)
        lon_at = spread(row[1:2] + row[3:4], lon_scale)
        near = [lat_taper(r, lat_at, lat_scale) * lon_taper(c, lon_at, lon_scale, dims[2]) for r, c in zip(rows, columns)]
        bits = [((mask >> block) & 1).astype(f32) for mask in masks]
        tiles = [out_ref[number] for number in range(len(rows))]
        new = update(lhs1_ref[block], lhs2_ref[block], tiles, lambda n: near[n], lambda n: bits[n])
        for number, tile in enumerate(new):
            out_ref[number] = tile

    def several(step, c):
        for number in range(4):
            assimilate(step * 4 + number)
        return c

    lax.fori_loop(0, blocks // 4, several, 0)


def own_kernel(dims, span, base, last, where_ref, count_ref, list_ref, obs_ref, lhs1_ref, lhs2_ref, x_ref, out_ref, loc_ref, *scratch):
    lat_scale, lon_scale = scales(dims)
    lat_dev, lon_dev, lon_total = dims
    lat_start, lon_start = where_ref[0], where_ref[1]
    state = scratch[0] if last else out_ref
    state[...] = x_ref[...]
    columns = (lon_start + lax.broadcasted_iota(i32, (LANES, LANES), 1)).astype(f32)

    def assimilate(block, carry):
        row = obs_ref[block]
        lat_at = spread(row[0:1] + row[2:3], lat_scale)
        own_lon = lon_taper(columns, spread(row[1:2] + row[3:4], lon_scale), lon_scale, lon_total)
        for a in range(lat_dev):
            loc_ref[a] = lat_taper((lat_start + a).astype(f32), lat_at, lat_scale) * own_lon

        def own(step, c):
            which = [list_ref[block, step * CHUNK + number] for number in range(CHUNK)]
            new = update(lhs1_ref[block - base], lhs2_ref[block - base], [state[w] for w in which],
                         lambda number: loc_ref[which[number] % lat_dev])
            for number in range(CHUNK):
                state[which[number]] = new[number]
            return c

        lax.fori_loop(0, pl.cdiv(count_ref[block], CHUNK), own, 0)
        return carry

    lax.fori_loop(span[0], span[1], assimilate, 0)
    if last:
        for slab in range(out_ref.shape[1]):
            out_ref[:, slab, :] = state[slab]


def word_kernel(slot_ref, table_ref, out_ref):
    for batch in range(slot_ref.shape[0]):
        slot = slot_ref[batch]
        place = slot % LANES
        row = slot // LANES
        result = jnp.zeros_like(slot)
        for number in range(table_ref.shape[1]):
            line = jnp.broadcast_to(table_ref[batch, number:number + 1], slot.shape)
            found = jnp.take_along_axis(line, place, axis=1)
            result = jnp.where(row == number, found, result)
        out_ref[batch] = result


def body(ensemble, obs_values, obs_error_var, obs_lat, obs_lon, obs_level, obs_frac, loc_mask):
    members, var_count, level_dev, lat_dev, lon_dev = ensemble.shape
    batches, blocks = loc_mask.shape[:2]
    obs_total = obs_values.shape[1]
    lat_parts, lon_parts, lev_parts = (lax.axis_size(name) for name in AXES)
    lat_at, lon_at, lev_at = (lax.axis_index(name) for name in AXES)
    lon_total, level_total, lat_total = lon_dev * lon_parts, level_dev * lev_parts, lat_dev * lat_parts
    lat_start, lon_start, level_start = lat_at * lat_dev, lon_at * lon_dev, lev_at * level_dev
    slabs = var_count * level_dev * lat_dev
    keep = (lat_at * lon_parts + lon_at) % blocks

    variable, level = obs_level // level_total, obs_level % level_total
    level_local = level - level_start
    cells, slots = [], []
    for row_step, col_step in ((0, 0), (1, 0), (0, 1), (1, 1)):
        row = obs_lat + row_step
        col = (obs_lon + col_step) % lon_total
        row_local, col_local = row - lat_start, col - lon_start
        held = (
            (level_local >= 0) & (level_local < level_dev) & (row_local >= 0) & (row_local < lat_dev)
            & (col_local >= 0) & (col_local < lon_dev)
        )
        cell = ((variable * level_dev + level_local) * lat_dev + row_local) * lon_dev + col_local
        cells.append(jnp.where(held, cell, -1))
        slots.append((obs_level * lat_total + row) * lon_parts + col // lon_dev)
    cells = jnp.stack(cells)
    slots = jnp.stack([slot.reshape(batches, blocks, LANES) for slot in slots], axis=2)
    spots = jnp.where(jnp.max(cells, axis=0) >= 0, jnp.arange(obs_total, dtype=i32), obs_total)
    grid = spots.reshape(batches, blocks, LANES)
    lane = jnp.arange(LANES)
    inside = jnp.min(jnp.where(lane[:, None] <= lane, grid[:, :, None, :], obs_total), axis=3)
    number = jnp.arange(blocks)
    beyond = jnp.min(jnp.where(number[:, None] < number, jnp.min(grid, axis=2)[:, None, :], obs_total), axis=2)
    nxt = jnp.minimum(inside, beyond[:, :, None]).reshape(batches, obs_total)
    nxt = jnp.concatenate([nxt, jnp.full((batches, 1), obs_total, i32)], axis=1)

    own = loc_mask.reshape(batches, blocks, slabs)
    count = jnp.sum(own, axis=2)
    rank = jnp.cumsum(own, axis=2) - 1
    padded = slabs + CHUNK
    hit = (rank[..., None] == jnp.arange(padded)) & (own[..., None] > 0)
    number = jnp.arange(slabs, dtype=i32)[:, None]
    active = slabs + jnp.sum(jnp.where(hit, number - slabs, 0), axis=2)

    def rows_of(values):
        return values.astype(f32).reshape(batches, blocks, LANES)

    obs_rows = jnp.stack(
        [rows_of(v) for v in (obs_lat, obs_lon, obs_frac[:, 0], obs_frac[:, 1], obs_values, obs_error_var,
                              (obs_lon + 1) % lon_total, obs_lat)],
        axis=2,
    )
    devices, tiles = lat_parts * lon_parts * lev_parts, 4 * blocks
    carry = tiles // devices if batches == 2 and tiles % devices == 0 and 4 % (tiles // devices) == 0 else 0
    first = ((lev_at * lat_parts + lat_at) * lon_parts + lon_at) * carry
    where = jnp.stack([lat_start, lon_start, keep, first % 4, lat_at, lon_at, lev_at]).astype(i32)

    def extended(values):
        ahead = lax.dynamic_index_in_dim(values[-1], first // 4, 0, True)
        more = jnp.concatenate([jnp.zeros_like(ahead), ahead], axis=0)
        return jnp.concatenate([values, jnp.broadcast_to(more, (batches,) + more.shape)], axis=1)

    obs_rows, slots = extended(obs_rows), extended(slots)
    smem = pl.BlockSpec(memory_space=pltpu.SMEM)
    vmem = pl.BlockSpec(memory_space=pltpu.VMEM)
    params = pltpu.CompilerParams(vmem_limit_bytes=56 * 1024 * 1024)
    state_shape = jax.ShapeDtypeStruct((slabs + 1, members, LANES), f32)
    natural_shape = jax.ShapeDtypeStruct((members, slabs, LANES), f32)

    def pick(which, x, natural):
        stencil_shape = jax.ShapeDtypeStruct((which.stop - which.start, blocks, 4, members, LANES), f32)
        return pl.pallas_call(
            pick_kernel,
            out_shape=(stencil_shape, state_shape) if natural else (stencil_shape,),
            in_specs=[smem, smem, vmem],
            out_specs=(vmem, vmem) if natural else (vmem,),
            compiler_params=params,
        )(nxt[which], cells[:, which], x)

    dims = (lat_dev, lon_dev, lon_total)

    def assimilate(batch, stencils):
        shapes = (
            jax.ShapeDtypeStruct((blocks, 2, LANES), f32),
            jax.ShapeDtypeStruct((2, LANES), f32),
            jax.ShapeDtypeStruct((blocks, LANES, 256), bf16),
            jax.ShapeDtypeStruct((blocks, 2 * members, 256), bf16),
        )
        return pl.pallas_call(
            functools.partial(stencil_kernel, dims, (lat_parts, lon_parts, lev_parts) if carry else None),
            out_shape=shapes,
            in_specs=[smem] + [vmem] * (2 + len(stencils)),
            out_specs=(vmem,) * len(shapes),
            scratch_shapes=[
                pltpu.VMEM((blocks + 1, 4, members, LANES), f32),
                pltpu.VMEM((2, LANES, LANES), f32),
            ],
            compiler_params=params,
        )(where, obs_rows[batch], words[batch], *stencils)

    def shaped(stencils):
        if carry:
            return [part.reshape(lat_parts * lon_parts, carry, members, LANES) for part in stencils]
        return [stencils.reshape(blocks, 4, members, LANES)]

    def gathered(rows, name):
        if not carry:
            return collect(rows, name).reshape(-1, LANES)
        return pieces(rows, name) if name == "lev" else jnp.concatenate(pieces(rows, name), axis=0)

    def bring(batch, share, factors):
        return pl.pallas_call(
            functools.partial(carry_kernel, dims),
            out_shape=jax.ShapeDtypeStruct((carry, members, LANES), f32),
            in_specs=[smem] + [vmem] * 5,
            out_specs=vmem,
            compiler_params=params,
        )(where, obs_rows[batch], words[batch], *factors, share.reshape(carry, members, LANES)).reshape(-1, LANES)

    def advance(batch, x, factors, span):
        last = batch == batches - 1 and span[1] == blocks
        size = 1
        while span[0] // size * size + size < span[1]:
            size *= 2
        size = min(size, blocks)
        at = span[0] // size

        def window(factor):
            return pl.BlockSpec((size,) + factor.shape[1:], lambda i: (at, 0, 0))

        def full(values):
            return pl.BlockSpec(values.shape, lambda i: (0,) * values.ndim)

        return pl.pallas_call(
            functools.partial(own_kernel, dims, span, at * size, last),
            grid=(1,),
            out_shape=natural_shape if last else state_shape,
            in_specs=[smem] * 3 + [full(obs_rows[batch]), window(factors[0]), window(factors[1]), full(x)],
            out_specs=full(natural_shape if last else state_shape),
            scratch_shapes=[pltpu.VMEM((lat_dev, LANES, LANES), f32)]
            + ([pltpu.VMEM(state_shape.shape, f32)] if last else []),
            compiler_params=params,
        )(where, count[batch], active[batch], obs_rows[batch], *factors, x)

    natural = ensemble.reshape(members, slabs, LANES)
    together = lax.optimization_barrier
    picked, x = pick(slice(0, 1), natural, True)
    share = share_sum(picked.reshape(1, -1, LANES), "lev")
    if carry:
        share, x = together((share, x))
        ahead = pick(slice(1, 2), x, False)[0].reshape(1, -1, LANES)
    share = share_sum(share, "lat")
    masks = loc_mask.reshape(batches * blocks, slabs)
    if carry:
        share, ahead, masks = together((share, ahead, masks))
        ahead = share_sum(ahead, "lev")
    share = share_sum(share, "lon")[0]
    masks = collect(masks, "lon")
    share, masks = together((share, masks))
    stencils = gathered(share, "lon")
    masks = collect(masks, "lat")
    stencils, masks = together((stencils, masks))
    stencils = gathered(stencils, "lat")
    masks = collect(masks, "lev").reshape(lev_parts, lat_parts, lon_parts, batches, blocks, slabs)
    bits = together(jnp.sum(masks << jnp.arange(blocks, dtype=i32)[:, None], axis=4))
    bits = bits.reshape(lev_parts, lat_parts, lon_parts, batches, var_count, level_dev, lat_dev)
    bits = bits.transpose(3, 4, 0, 5, 1, 6, 2).reshape(batches, -1)
    bits = jnp.pad(bits, ((0, 0), (0, -bits.shape[1] % LANES))).reshape(batches, -1, LANES)
    words = pl.pallas_call(
        word_kernel,
        out_shape=jax.ShapeDtypeStruct((batches, (blocks + 2) * 4, LANES), i32),
        in_specs=[vmem, vmem],
        out_specs=vmem,
    )(slots.reshape(batches, -1, LANES), bits).reshape(batches, blocks + 2, 4, LANES)
    if carry:
        stencils, ahead, words = together((stencils, ahead, words))
    stencils = gathered(stencils, "lev")
    if carry:
        stencils, ahead = together((stencils, ahead))
    prior_parts, post_parts = [], []
    for batch in range(batches):
        prior, post, *factors = assimilate(batch, shaped(stencils))
        prior_parts.append(prior.transpose(1, 0, 2).reshape(2, obs_total))
        post_parts.append(post)
        if batch == batches - 1:
            rows, names, cuts = jnp.concatenate(post_parts, axis=0), ("lon", "lat"), (0, blocks // 2, blocks)
        elif carry:
            ahead = share_sum(ahead, "lat")
            ahead, factors = together((ahead, factors))
            ahead = share_sum(ahead, "lon")
            x = advance(batch, x, factors, (0, blocks // 4))
            ahead, x = together((ahead, x))
            rows = bring(batch, ahead, factors)
            names, cuts = ("lon", "lat", "lev"), (blocks // 4, blocks // 2, blocks * 7 // 8, blocks)
        else:
            x = advance(batch, x, factors, (0, blocks))
            stencils = whole_of(share_of(pick(slice(batch + 1, batch + 2), x, False)[0])[0])
            continue
        for name, start, stop in zip(names, cuts, cuts[1:]):
            if batch == batches - 1:
                rows = collect(rows, name).reshape(-1, LANES)
            else:
                rows = gathered(rows, name)
            x = advance(batch, x, factors, (start, stop))
            rows, x = together((rows, x))
        stencils = rows
    posts = stencils.reshape(-1, 2 * batches, LANES)[:blocks]
    posts = posts.transpose(1, 0, 2).reshape(batches, 2, obs_total)
    return x.reshape(ensemble.shape), jnp.stack(prior_parts), posts


def solution(mesh):
    state = P(None, None, "lev", "lat", "lon")
    return jax.shard_map(
        body,
        mesh=mesh,
        in_specs=(state, P(), P(), P(), P(), P(), P(), P(None, None, None, "lev", "lat", "lon")),
        out_specs=(state, P(), P()),
        check_vma=False,
    )
```
